32 devices in a mesh: dp: 16 (over z, y, x), tensor: 2 (over core).
Axes of the slice: x: 2, y: 2, z: 4, core: 2. Of those that a mesh axis runs over, the one named last changes fastest.
Arguments:
- patches_in: bfloat16 [64, 256, 768], P(('dp', 'tensor')), may hold values from -6 to 6
- cotangent: bfloat16 [64, 256, 768], P(('dp', 'tensor')), may hold values from -6 to 6
- condition: float32 [64, 768], replicated, may hold values from -6 to 6
- frame_clip: int32 [64], P('dp'), may hold values from 0 to 63, as said below
- frame_valid: int32 [64], P('dp'), may hold values from 0 to 1, as said below
- w_ada: bfloat16 [768, 6912], replicated, may hold values from -0.21875 to 0.21875
- sp_qkv: bfloat16 [3, 768, 768], P(None, None, 'tensor'), may hold values from -0.21875 to 0.21875
- sp_out: bfloat16 [768, 768], P('tensor'), may hold values from -2 to 2
- tm_qkv: bfloat16 [3, 768, 768], P(None, None, 'tensor'), may hold values from -0.21875 to 0.21875
- tm_out: bfloat16 [768, 768], P('tensor'), may hold values from -0.3125 to 0.3125
- w_up: bfloat16 [768, 3072], P(None, 'tensor'), may hold values from -0.21875 to 0.21875
- w_down: bfloat16 [3072, 768], P('tensor'), may hold values from -0.109375 to 0.109375
Outputs:
- patches_out: bfloat16 [64, 256, 768], P(('dp', 'tensor'))
- patches_in_grad: float32 [64, 256, 768], P(('dp', 'tensor'))
- condition_grad: float32 [64, 768], P(None, ('dp', 'tensor'))
- ada_grad: float32 [768, 6912], P(None, ('dp', 'tensor'))
- sp_qkv_grad: float32 [3, 768, 768], P(None, 'dp', 'tensor')
- sp_out_grad: float32 [768, 768], P('tensor', 'dp')
- tm_qkv_grad: float32 [3, 768, 768], P(None, 'dp', 'tensor')
- tm_out_grad: float32 [768, 768], P('tensor', 'dp')
- up_grad: float32 [768, 3072], P('dp', 'tensor')
- down_grad: float32 [3072, 768], P('tensor', 'dp')
The draws below stay inside these ranges and needn't reach their ends.
Inputs may be any that keep to these rules, and one draw needn't show every extreme that they name: `frame_clip`: within the 4 frame slots of one dp group, slots of one clip are consecutive; no clip number appears in two groups; slot 0 of group 0 holds clip 64 - 1. `frame_valid`: in each group of 4 slots the real frames come first, at least 2 of them; some group is full.
All inputs are finite; a program needn't handle non-finite values.
Results may differ from the reference program's by a relative error of at most 0.017.
Values may be sent and summed in bfloat16 or wider, within the bound.
No kernel may reach another device: no remote copies, remote signals or barrier semaphores. Data moves between devices by JAX's collectives and lax.ppermute only.
A program may use at most 192 MiB of HBM per device.

```python
import jax
import jax.numpy as jnp
from jax import lax

D = 768
H = 12
HD = 64
FF = 3072
P_SIZE = 256
FG = 4
FRAMES = 64
CLIPS = 64


def clip_layout(key):
    groups = FRAMES // FG
    key_cut, key_count, key_full, key_perm = jax.random.split(key, 4)
    boundary = jax.random.randint(key_cut, (groups, FG), 0, 3) == 0
    boundary = boundary.at[:, 0].set(True)
    position = jnp.cumsum(boundary.astype(jnp.int32), axis=1) - 1
    counts = jax.random.randint(key_count, (groups,), FG // 2, FG + 1)
    full_group = jax.random.randint(key_full, (), 0, groups)
    counts = jnp.where(jnp.arange(groups) == full_group, FG, counts)
    valid_rows = (jnp.arange(FG)[None, :] < counts[:, None]).astype(jnp.int32)
    shuffled = jax.random.permutation(key_perm, FRAMES - 1).astype(jnp.int32)
    shuffled = jnp.concatenate([jnp.full((1,), FRAMES - 1, jnp.int32), shuffled])
    clip_ids = shuffled[jnp.arange(groups)[:, None] * FG + position]
    return (clip_ids.reshape(FRAMES).astype(jnp.int32), valid_rows.reshape(FRAMES))


def draw_frame_clip(key, part):
    return clip_layout(key)[0]


def draw_frame_valid(key, part):
    return clip_layout(key)[1]


def block_levels(rng, extent, shards, low, top_value):
    loudness, own = 1.0, jax.random.fold_in(rng, 6)
    for axis_at, shards_of in shards:
        heights = jnp.exp(jax.random.uniform(jax.random.fold_in(own, axis_at), (shards_of,), jnp.float32, low / len(shards), top_value / len(shards)))
        loudness = loudness * jnp.repeat(heights, extent[axis_at] // shards_of).reshape([-1 if axis == axis_at else 1 for axis in range(len(extent))])
    return loudness


def noise(stream_key, shape, width, most, cuts=(), kind=jnp.bfloat16):
    loudness = block_levels(stream_key, shape, cuts, -0.22, 0.18) if cuts else 1.0
    array = jax.random.normal(stream_key, shape, jnp.float32) * width * loudness
    return jnp.minimum(jnp.maximum(array, -most), most).astype(kind)


def setup_inputs(seed: int = 0) -> dict:
    key_of = jax.random.split(jax.random.key(seed), 13)
    patches_in = noise(key_of[0], (FRAMES, P_SIZE, D), 1.0, 6.0, ((0, 32),))
    cotangent = noise(key_of[1], (FRAMES, P_SIZE, D), 1.0, 6.0, ((0, 32),))
    condition = noise(key_of[2], (CLIPS, D), 1.0, 6.0, (), jnp.float32)
    frame_clip = draw_frame_clip(jax.random.fold_in(key_of[12], 71), 0)
    frame_valid = draw_frame_valid(jax.random.fold_in(key_of[12], 71), 0)
    w_ada = noise(key_of[5], (D, 9 * D), D ** -0.5, 0.21875)
    sp_qkv = noise(key_of[6], (3, D, D), D ** -0.5, 0.21875, ((2, 2),))
    sp_out = noise(key_of[7], (D, D), (max(1, 3 * D // P_SIZE)) ** -0.5, 2.0, ((0, 2),))
    tm_qkv = noise(key_of[8], (3, D, D), D ** -0.5, 0.21875, ((2, 2),))
    tm_out = noise(key_of[9], (D, D), (D // 2) ** -0.5, 0.3125, ((0, 2),))
    w_up = noise(key_of[10], (D, FF), D ** -0.5, 0.21875, ((1, 2),))
    w_down = noise(key_of[11], (FF, D), FF ** -0.5, 0.109375, ((0, 2),))
    return dict(patches_in=patches_in, cotangent=cotangent, condition=condition, frame_clip=frame_clip, frame_valid=frame_valid, w_ada=w_ada, sp_qkv=sp_qkv, sp_out=sp_out, tm_qkv=tm_qkv, tm_out=tm_out, w_up=w_up, w_down=w_down)


@jax.custom_vjp
def low(v):
    return lax.optimization_barrier(v.astype(jnp.bfloat16)).astype(jnp.float32)

@jax.custom_vjp
def low_back(v):
    return v

def low_keep(v):
    return (low(v), None)

def low_pass(kept, grad):
    return (grad,)

def back_keep(v):
    return (v, None)

def back_low(kept, grad):
    return (low(grad),)
low.defvjp(low_keep, low_pass)
low_back.defvjp(back_keep, back_low)
highest = lax.Precision.HIGHEST
epsilon = 1e-06

def both_ways(value):
    return low_back(low(value))

def layer_norm(stream):
    centred = stream - lax.optimization_barrier(jnp.mean(stream, -1, keepdims=True))
    variance = lax.optimization_barrier(jnp.mean(centred * centred, -1, keepdims=True))
    return centred * lax.rsqrt(variance + epsilon)

def spatial_branch(sub_input, qkv_weight, out_weight):
    frame_n, patch_n = (sub_input.shape[0], sub_input.shape[1])
    qkv_all = both_ways(jnp.einsum('fpd,kdc->kfpc', sub_input, qkv_weight, precision=highest))
    qkv_all = qkv_all.reshape(3, frame_n, patch_n, H, HD)
    scores = low_back(jnp.einsum('fphd,fqhd->fhpq', qkv_all[0], qkv_all[1], precision=highest) * HD ** (-0.5))
    probs_low = low(jax.nn.softmax(scores, axis=-1))
    context = jnp.einsum('fhpq,fqhd->fphd', probs_low, qkv_all[2], precision=highest)
    context = both_ways(context.reshape(frame_n, patch_n, D))
    return low_back(jnp.einsum('fpc,cd->fpd', context, out_weight, precision=highest))

def temporal_branch(sub_input, qkv_weight, out_weight, allowed):
    frame_n, patch_n = (sub_input.shape[0], sub_input.shape[1])
    qkv_all = both_ways(jnp.einsum('fpd,kdc->kfpc', sub_input, qkv_weight, precision=highest))
    qkv_all = qkv_all.reshape(3, frame_n, patch_n, H, HD)
    scores = low_back(jnp.einsum('fphd,gphd->phfg', qkv_all[0], qkv_all[1], precision=highest) * HD ** (-0.5))
    scores = jnp.where(allowed, scores, -1e+30)
    probs_low = low(jax.nn.softmax(scores, axis=-1))
    context = jnp.einsum('phfg,gphd->fphd', probs_low, qkv_all[2], precision=highest)
    context = both_ways(context.reshape(frame_n, patch_n, D))
    return low_back(jnp.einsum('fpc,cd->fpd', context, out_weight, precision=highest))

def mlp_branch(sub_input, up_weight, down_weight):
    pre_act = low_back(jnp.einsum('fpd,dc->fpc', sub_input, up_weight, precision=highest))
    hidden_act = low(jax.nn.gelu(pre_act, approximate=True))
    return low_back(jnp.einsum('fpc,cd->fpd', hidden_act, down_weight, precision=highest))

def group_layer(pieces, mod_all, weight_set):
    stream, clip_ids, valid_rows = pieces
    mods = mod_all[clip_ids].reshape(clip_ids.shape[0], 9, 1, D)
    valid_mask = valid_rows[:, None, None]
    allowed = (clip_ids[:, None] == clip_ids[None, :]) & (valid_rows[None, :] > 0.5) | jnp.eye(clip_ids.shape[0], dtype=bool)
    for branch_idx in range(3):
        sub_input = low(layer_norm(stream) * (1.0 + mods[:, 3 * branch_idx + 1]) + mods[:, 3 * branch_idx])
        inner_weight = weight_set[2 * branch_idx]
        outer_weight = weight_set[2 * branch_idx + 1]
        if branch_idx == 0:
            branch_out = spatial_branch(sub_input, inner_weight, outer_weight)
        elif branch_idx == 1:
            branch_out = temporal_branch(sub_input, inner_weight, outer_weight, allowed)
        else:
            branch_out = mlp_branch(sub_input, inner_weight, outer_weight)
        stream = stream + valid_mask * mods[:, 3 * branch_idx + 2] * branch_out
    return stream

def as_float(value):
    return value.astype(jnp.float32)

def reference(patches_in, cotangent, condition, frame_clip, frame_valid, w_ada, sp_qkv, sp_out, tm_qkv, tm_out, w_up, w_down):
    groups = FRAMES // FG
    clip_groups = frame_clip.reshape(groups, FG)
    valid_groups = frame_valid.astype(jnp.float32).reshape(groups, FG)

    def forward(stream_in, cond_in, ada_in, sq_in, so_in, tq_in, to_in, up_in, down_in):
        mod_all = jnp.dot(low(jax.nn.silu(cond_in)), ada_in, precision=highest)
        weight_set = (sq_in, so_in, tq_in, to_in, up_in, down_in)

        def one_group(pieces):
            return group_layer(pieces, mod_all, weight_set)
        outputs = lax.map(jax.checkpoint(one_group), (stream_in.reshape(groups, FG, P_SIZE, D), clip_groups, valid_groups))
        return outputs.reshape(FRAMES, P_SIZE, D)
    result, pullback = jax.vjp(forward, as_float(patches_in), as_float(condition), as_float(w_ada), as_float(sp_qkv), as_float(sp_out), as_float(tm_qkv), as_float(tm_out), as_float(w_up), as_float(w_down))
    grads = pullback(as_float(cotangent))
    return (result.astype(jnp.bfloat16), grads[0], grads[1], grads[2], grads[3], grads[4], grads[5], grads[6], grads[7], grads[8])
```

```python
import jax
import jax.numpy as jnp
from jax import lax
from jax.sharding import PartitionSpec as P

HD = 64
f32 = jnp.float32
bf16 = jnp.bfloat16
highest = lax.Precision.HIGHEST
epsilon = 1e-06
spatial_forms = ("fphd,fqhd->fhpq", "fhpq,fqhd->fphd", "fhpq,fphd->fqhd")
temporal_forms = ("fphd,gphd->phfg", "phfg,gphd->fphd", "phfg,fphd->gphd")


def mm(form, a, b):
    return jnp.einsum(form, a, b, preferred_element_type=f32)


def layer_norm(stream):
    centred = stream - jnp.mean(stream, -1, keepdims=True)
    variance = jnp.mean(centred * centred, -1, keepdims=True)
    inv_std = lax.rsqrt(variance + epsilon)
    return centred * inv_std, inv_std


def norm_backward(input_grad, normed, inv_std, scale1):
    normed_grad = input_grad * scale1
    return inv_std * (
        normed_grad
        - jnp.mean(normed_grad, -1, keepdims=True)
        - normed * jnp.mean(normed_grad * normed, -1, keepdims=True)
    )


def heads_of(a):
    return a.reshape(a.shape[:-1] + (a.shape[-1] // HD, HD))


def flat(a):
    return a.reshape(a.shape[:-2] + (-1,))


def gelu_tanh(value):
    return jax.nn.gelu(value, approximate=True)


def attention_forward(forms, sub, inner, outer, allowed):
    branch, kept = 0.0, []
    for w_in, w_out in zip(inner, outer):
        q, k, v = (heads_of(mm("fpd,dc->fpc", sub, w_in[i]).astype(bf16)) for i in range(3))
        scores = mm(forms[0], q, k) * HD ** (-0.5)
        if allowed is not None:
            scores = jnp.where(allowed, scores, -1e30)
        probs = jax.nn.softmax(scores, axis=-1).astype(bf16)
        context = flat(mm(forms[1], probs, v).astype(bf16))
        branch = branch + mm("fpc,cd->fpd", context, w_out)
        kept.append((q, k, v, probs, context))
    return branch, kept


def attention_backward(forms, sub, inner, outer, kept, rows):
    input_grad, inner_grads, outer_grads = 0.0, [], []
    for w_in, w_out, (q, k, v, probs, context) in zip(inner, outer, kept):
        outer_grads.append(mm("fpd,fpc->dc", rows, context))
        context_grad = heads_of(mm("fpd,cd->fpc", rows, w_out).astype(bf16))
        prob_grad = mm(forms[0], context_grad, v)
        value_grad = mm(forms[2], probs, context_grad)
        p32 = probs.astype(f32)
        score_grad = (p32 * (prob_grad - jnp.sum(prob_grad * p32, -1, keepdims=True))).astype(bf16)
        query_grad = mm(forms[1], score_grad, k) * HD ** (-0.5)
        key_grad = mm(forms[2], score_grad, q) * HD ** (-0.5)
        grads = [flat(g).astype(bf16) for g in (query_grad, key_grad, value_grad)]
        inner_grads.append(jnp.concatenate([mm("fpd,fpc->dc", sub, g) for g in grads], axis=1))
        for i in range(3):
            input_grad = input_grad + mm("fpc,dc->fpd", grads[i], w_in[i])
    return input_grad, inner_grads, outer_grads


def local(
    patches_in, cotangent, condition, frame_clip, frame_valid, w_ada, sp_qkv, sp_out, tm_qkv, tm_out, w_up, w_down,
    dp_size,
):
    frames, patches, width = patches_in.shape
    half = patches // 2
    clips = condition.shape[0]
    t = lax.axis_index("tensor")
    d = lax.axis_index("dp")
    first = t == 0

    def swap(a):
        return lax.ppermute(a, "tensor", [(0, 1), (1, 0)])

    def to_patch_split(a):
        own = lax.dynamic_slice_in_dim(a, t * half, half, 1)
        other = lax.dynamic_slice_in_dim(a, (1 - t) * half, half, 1)
        return jnp.concatenate([own, swap(other)], axis=0)

    def to_frame_split(a, sent):
        own, received = a[:frames], swap(sent)
        return jnp.where(
            first, jnp.concatenate([own, received], axis=1), jnp.concatenate([received, own], axis=1)
        )

    def own_first(a):
        return jnp.where(first, a, jnp.concatenate([a[frames:], a[:frames]], axis=0))

    sq, so, tq, to, up, dn = (
        (w, swap(w)) for w in (sp_qkv, sp_out, tm_qkv, tm_out, w_up, w_down)
    )
    clip_ids = own_first(frame_clip)
    valid_ids = own_first(frame_valid)
    onehot = (clip_ids[:, None] == jnp.arange(clips, dtype=jnp.int32)[None, :]).astype(f32)
    cond_rows = jnp.dot(onehot, condition, precision=highest)
    act_low = jax.nn.silu(cond_rows).astype(bf16)
    mods = jnp.dot(act_low, w_ada, preferred_element_type=f32).reshape(2 * frames, 9, 1, width)
    valid = valid_ids.astype(f32)[:, None, None]
    shift = [mods[:, 3 * b] for b in range(3)]
    scale1 = [1.0 + mods[:, 3 * b + 1] for b in range(3)]
    gate = [valid * mods[:, 3 * b + 2] for b in range(3)]
    allowed = (clip_ids[:, None] == clip_ids[None, :]) & (valid_ids[None, :] == 1) | jnp.eye(
        2 * frames, dtype=bool
    )
    x_split = to_patch_split(patches_in)
    c_split = to_patch_split(cotangent)

    n0, r0 = layer_norm(patches_in.astype(f32))
    sub0 = (n0 * scale1[0][:frames] + shift[0][:frames]).astype(bf16)
    branch0, kept0 = attention_forward(spatial_forms, sub0, sq, so, None)
    branch0 = branch0.astype(bf16)
    stream1 = x_split.astype(f32) + gate[0] * to_patch_split(branch0).astype(f32)
    n1, r1 = layer_norm(stream1)
    sub1 = (n1 * scale1[1] + shift[1]).astype(bf16)
    branch1, kept1 = attention_forward(temporal_forms, sub1, tq, to, allowed)
    stream2 = stream1 + gate[1] * branch1
    n2, r2 = layer_norm(stream2)
    sub2 = (n2 * scale1[2] + shift[2]).astype(bf16)
    grad = c_split.astype(f32)
    rows2 = (gate[2] * grad).astype(bf16)
    branch2, in2, up_grads, down_grads = 0.0, 0.0, [], []
    for w_in, w_out in zip(up, dn):
        pre = mm("fpd,dc->fpc", sub2, w_in)
        act, back = jax.vjp(gelu_tanh, pre)
        act = act.astype(bf16)
        branch2 = branch2 + mm("fpc,cd->fpd", act, w_out)
        down_grads.append(mm("fpd,fpc->dc", rows2, act))
        pre_grad = back(mm("fpd,cd->fpc", rows2, w_out))[0].astype(bf16)
        up_grads.append(mm("fpd,fpc->dc", sub2, pre_grad))
        in2 = in2 + mm("fpc,dc->fpd", pre_grad, w_in)
    out_split = (stream2 + gate[2] * branch2).astype(bf16)
    patches_out = to_frame_split(out_split, out_split[frames:])
    mod = [None] * 9
    mod[8] = jnp.sum(valid * branch2 * grad, axis=1)
    mod[6] = jnp.sum(in2, axis=1)
    mod[7] = jnp.sum(in2 * n2, axis=1)
    grad = grad + norm_backward(in2, n2, r2, scale1[2])
    mod[5] = jnp.sum(valid * branch1 * grad, axis=1)
    rows1 = (gate[1] * grad).astype(bf16)
    in1, tq_grads, to_grads = attention_backward(temporal_forms, sub1, tq, to, kept1, rows1)
    mod[3] = jnp.sum(in1, axis=1)
    mod[4] = jnp.sum(in1 * n1, axis=1)
    grad = grad + norm_backward(in1, n1, r1, scale1[1])
    delta = (grad - c_split.astype(f32)).astype(bf16)
    grad = cotangent.astype(f32) + to_frame_split(delta, delta[frames:]).astype(f32)
    mod[2] = jnp.sum(valid[:frames] * branch0.astype(f32) * grad, axis=1)
    rows0 = (gate[0][:frames] * grad).astype(bf16)
    in0, sq_grads, so_grads = attention_backward(spatial_forms, sub0, sq, so, kept0, rows0)
    mod[0] = jnp.sum(in0, axis=1)
    mod[1] = jnp.sum(in0 * n0, axis=1)
    grad = grad + norm_backward(in0, n0, r0, scale1[0][:frames])

    bit0, bit1, rest = d % 2, d // 2 % 2, d // 4
    outer = dp_size // 4

    def both_cores(first_bit, second_bit):
        return [(2 * i, 2 * (i ^ first_bit)) for i in range(dp_size)] + [
            (2 * i + 1, 2 * (i ^ second_bit) + 1) for i in range(dp_size)
        ]

    def pick(a, axis, at):
        return lax.dynamic_index_in_dim(a, at, axis, keepdims=False)

    def reduce_dp(own, other):
        total = (own + swap(other.astype(bf16)).astype(f32)).astype(bf16)
        columns = total.shape[1]
        a = total.reshape(outer, 2, 2, width // dp_size, columns)
        keep = jnp.where(first, pick(a, 2, bit0), pick(a, 1, bit1))
        send = jnp.where(first, pick(a, 2, 1 - bit0), pick(a, 1, 1 - bit1))
        b = keep + lax.ppermute(send, ("dp", "tensor"), both_cores(1, 2))
        bit = jnp.where(first, bit1, bit0)
        keep, send = pick(b, 1, bit), pick(b, 1, 1 - bit)
        c = keep + lax.ppermute(send, ("dp", "tensor"), both_cores(2, 1))
        if outer != 4:
            groups = [[4 * z + i for z in range(outer)] for i in range(4)]
            return lax.psum_scatter(
                c.astype(f32), "dp", scatter_dimension=0, axis_index_groups=groups, tiled=False
            )
        total = pick(c, 0, rest).astype(f32)
        for k in range(1, outer):
            piece = pick(c, 0, (rest + k) % outer)
            total = total + lax.ppermute(
                piece, "dp", [(i, (i + 4 * k) % dp_size) for i in range(dp_size)]
            ).astype(f32)
        return total

    up_out = reduce_dp(*up_grads)
    down_out = reduce_dp(*down_grads).T
    tq_out = reduce_dp(*tq_grads)
    to_out = reduce_dp(*to_grads).T
    sq_out = reduce_dp(*sq_grads)
    so_out = reduce_dp(*so_grads).T

    def three(a):
        return a.reshape(a.shape[0], 3, -1).transpose(1, 0, 2)

    shared = jnp.stack(mod[3:], axis=1).reshape(2 * frames, -1)
    late = jnp.stack(mod[:3], axis=1).reshape(frames, -1)
    mine = jnp.concatenate([late, shared[:frames] + swap(shared[frames:])], axis=1)
    hi = mine.astype(bf16)
    mid = (mine - hi.astype(f32)).astype(bf16)
    low = (mine - hi.astype(f32) - mid.astype(f32)).astype(bf16)
    parts = jnp.concatenate([hi, mid, low], axis=0)
    act_grad = lax.dot_general(parts, w_ada, (((1,), (1,)), ((), ())), preferred_element_type=f32)
    act_grad = act_grad[:frames] + act_grad[frames : 2 * frames] + act_grad[2 * frames :]
    unused, silu_back = jax.vjp(jax.nn.silu, cond_rows[:frames])
    cond_term = silu_back(act_grad)[0]
    devices = 2 * dp_size
    own_ids = clip_ids[:frames].astype(f32)
    payload = jnp.concatenate(
        [
            mine.reshape(frames, devices, -1),
            cond_term.reshape(frames, devices, -1),
            jnp.broadcast_to(own_ids[:, None, None], (frames, devices, 1)),
        ],
        axis=2,
    )
    got = lax.all_to_all(
        payload.transpose(1, 0, 2), ("dp", "tensor"), split_axis=0, concat_axis=0, tiled=True
    ).reshape(devices * frames, -1)
    ada_cols = 9 * width // devices
    ids = got[:, -1].astype(jnp.int32)
    every = (ids[:, None] == jnp.arange(clips, dtype=jnp.int32)[None, :]).astype(f32)
    act_all = jnp.dot(
        every, jax.nn.silu(condition).astype(bf16).astype(f32), precision=highest
    )
    ada_grad = jnp.dot(act_all.T, got[:, :ada_cols], precision=highest)
    condition_grad = jnp.dot(every.T, got[:, ada_cols:-1], precision=highest)
    return (
        patches_out, grad, condition_grad, ada_grad, three(sq_out), so_out, three(tq_out), to_out, up_out, down_out,
    )


def solution(mesh):
    dp_size = mesh.shape["dp"]

    def body(*args):
        return local(*args, dp_size=dp_size)

    return jax.shard_map(
        body,
        mesh=mesh,
        in_specs=(
            P(("dp", "tensor"), None, None),
            P(("dp", "tensor"), None, None),
            P(),
            P("dp"),
            P("dp"),
            P(),
            P(None, None, "tensor"),
            P("tensor", None),
            P(None, None, "tensor"),
            P("tensor", None),
            P(None, "tensor"),
            P("tensor", None),
        ),
        out_specs=(
            P(("dp", "tensor"), None, None),
            P(("dp", "tensor"), None, None),
            P(None, ("dp", "tensor")),
            P(None, ("dp", "tensor")),
            P(None, "dp", "tensor"),
            P("tensor", "dp"),
            P(None, "dp", "tensor"),
            P("tensor", "dp"),
            P("dp", "tensor"),
            P("tensor", "dp"),
        ),
        check_vma=False,
    )
```

```python
import functools

import jax
import jax.numpy as jnp
from jax import lax
from jax.experimental import pallas as pl
from jax.experimental.pallas import tpu as pltpu
from jax.sharding import PartitionSpec as P

HD = 64
LANES = 128
SCALE = HD**-0.5
f32 = jnp.float32
bf16 = jnp.bfloat16
highest = lax.Precision.HIGHEST
epsilon = 1e-06
VMEM_LIMIT = 60 * 2**20
NN = (((1,), (0,)), ((), ()))
NT = (((1,), (1,)), ((), ()))
TN = (((0,), (0,)), ((), ()))
VM = pl.BlockSpec(memory_space=pltpu.VMEM)
SM = pl.BlockSpec(memory_space=pltpu.SMEM)
shape = jax.ShapeDtypeStruct


def dot(a, b, dims=NN):
    return lax.dot_general(a, b, dims, preferred_element_type=f32)


def norm(x):
    centred = x - jnp.mean(x, -1, keepdims=True)
    inv_std = lax.rsqrt(jnp.mean(centred * centred, -1, keepdims=True) + epsilon)
    return centred * inv_std, inv_std


def norm_back(input_grad, normed, inv_std, scale1):
    d = input_grad * scale1
    return inv_std * (
        d - jnp.mean(d, -1, keepdims=True) - normed * jnp.mean(d * normed, -1, keepdims=True)
    )


def column_sum(x):
    return jnp.sum(x, 0, keepdims=True)


def whole(dims):
    return pl.BlockSpec(dims, lambda *at: (0,) * len(dims))


def call(kernel, flops, bytes_accessed, exps=0, **options):
    return pl.pallas_call(
        kernel,
        compiler_params=pltpu.CompilerParams(vmem_limit_bytes=VMEM_LIMIT),
        cost_estimate=pl.CostEstimate(
            flops=flops, bytes_accessed=bytes_accessed, transcendentals=exps
        ),
        **options,
    )


def head_masks():
    lane = lax.broadcasted_iota(jnp.int32, (1, LANES), 1)
    return [(lane < HD).astype(bf16), (lane >= HD).astype(bf16)]


def project(sub, weights, qkv, rows=slice(None)):
    cols = weights[0].shape[2]
    for h, w in enumerate(weights):
        for i in range(3):
            y = dot(sub, w[i])
            if i == 0:
                y = y * SCALE
            qkv[i, rows, h * cols : (h + 1) * cols] = y.astype(bf16)


def spatial_kernel(x, mod, wi0, wi1, wo0, wo1, sub, qkv, probs, ctx, branch):
    width, cols = x.shape[1], wi0.shape[2]
    normed, _ = norm(x[...].astype(f32))
    sub[...] = (normed * mod[0, 1:2] + mod[0, 0:1]).astype(bf16)
    project(sub[...], (wi0, wi1), qkv)
    masks = head_masks()

    def pair(j, carry):
        at = pl.ds(pl.multiple_of(j * LANES, LANES), LANES)
        q, k, v = qkv[0, :, at], qkv[1, :, at], qkv[2, :, at]
        out = 0.0
        for a in range(2):
            scores = dot(q * masks[a], k, NT)
            e = jnp.exp(scores - jnp.max(scores, -1, keepdims=True))
            p = (e * (1.0 / jnp.sum(e, -1, keepdims=True))).astype(bf16)
            probs[2 * j + a] = p
            out = out + dot(p, v * masks[a])
        ctx[:, at] = out.astype(bf16)
        return carry

    lax.fori_loop(0, width // LANES, pair, 0, unroll=3)
    branch[...] = (dot(ctx[:, :cols], wo0[...]) + dot(ctx[:, cols:], wo1[...])).astype(bf16)


def spatial(x, mod, wi, wo):
    frames = mod.shape[0]
    rows, width = x.shape
    n, heads = rows // frames, width // HD
    tokens = pl.BlockSpec((n, width), lambda f: (f, 0))
    return call(
        spatial_kernel,
        rows * width * (8 * width + 4 * n),
        8 * width * width + 20 * rows * width,
        frames * heads * n * n,
        grid=(frames,),
        in_specs=[tokens, pl.BlockSpec((1,) + mod.shape[1:], lambda f: (f, 0, 0))]
        + [whole(w.shape) for w in (*wi, *wo)],
        out_specs=[
            tokens,
            pl.BlockSpec((3, n, width), lambda f: (0, f, 0)),
            pl.BlockSpec((heads, n, n), lambda f: (f, 0, 0)),
            tokens,
            tokens,
        ],
        out_shape=[
            shape((rows, width), bf16),
            shape((3, rows, width), bf16),
            shape((frames * heads, n, n), bf16),
            shape((rows, width), bf16),
            shape((rows, width), bf16),
        ],
    )(x, mod, *wi, *wo)


def spatial_back_kernel(
    grad, mod, sub, qkv, probs, ctx, branch, wo0, wo1, dqkv, own, other, dgate, rows
):
    f, frames = pl.program_id(0), pl.num_programs(0)
    width, cols, n = sub.shape[1], wo0.shape[0], probs.shape[1]
    here = pl.ds(pl.multiple_of(f * n, n), n)
    g = grad[...]
    dgate[...] = (column_sum(g * branch[...].astype(f32)) * mod[0, 3:4])[None]
    r = (g * mod[0, 2:3]).astype(bf16)
    rows[here, :] = r
    masks = head_masks()
    context_grad = [dot(r, w[...], NT).astype(bf16) for w in (wo0, wo1)]
    for j in range(width // LANES):
        at = slice(j * LANES, (j + 1) * LANES)
        h, low = divmod(j * LANES, cols)
        q, k, v = qkv[0, here, at], qkv[1, here, at], qkv[2, here, at]
        d = context_grad[h][:, low : low + LANES]
        product = d.astype(f32) * ctx[here, at].astype(f32)
        dq = dk = dv = 0.0
        for a in range(2):
            da = d * masks[a]
            p = probs[2 * j + a]
            delta = jnp.sum(product * masks[a].astype(f32), -1, keepdims=True)
            ds = (p.astype(f32) * (dot(da, v, NT) - delta)).astype(bf16)
            dv = dv + dot(p, da, TN)
            dq = dq + dot(ds, k * masks[a])
            dk = dk + dot(ds, q * masks[a], TN)
        dqkv[0, here, at] = (dq * SCALE).astype(bf16)
        dqkv[1, here, at] = dk.astype(bf16)
        dqkv[2, here, at] = dv.astype(bf16)

    @pl.when(f == frames - 1)
    def _():
        for h, out in ((1, other), (0, own)):
            at = slice(h * cols, (h + 1) * cols)
            for i in range(3):
                out[:, i * cols : (i + 1) * cols] = dot(sub[...], dqkv[i, :, at], TN).astype(bf16)
            out[:, 3 * cols :] = dot(rows[...], ctx[:, at], TN).astype(bf16)


def spatial_back(grad, mod, sub, qkv, probs, ctx, branch, wo):
    frames = mod.shape[0]
    rows, width = sub.shape
    n, heads, cols = rows // frames, width // HD, wo[0].shape[0]
    tokens = pl.BlockSpec((n, width), lambda f: (f, 0))
    return call(
        spatial_back_kernel,
        rows * width * (10 * width + 10 * n),
        8 * width * width + 24 * rows * width,
        grid=(frames,),
        in_specs=[
            tokens,
            pl.BlockSpec((1,) + mod.shape[1:], lambda f: (f, 0, 0)),
            whole(sub.shape),
            whole(qkv.shape),
            pl.BlockSpec((heads, n, n), lambda f: (f, 0, 0)),
            whole(ctx.shape),
            tokens,
            whole(wo[0].shape),
            whole(wo[1].shape),
        ],
        out_specs=[
            whole((3, rows, width)),
            whole((width, 4 * cols)),
            whole((width, 4 * cols)),
            pl.BlockSpec((1, 1, width), lambda f: (f, 0, 0)),
        ],
        out_shape=[
            shape((3, rows, width), bf16),
            shape((width, 4 * cols), bf16),
            shape((width, 4 * cols), bf16),
            shape((frames, 1, width), f32),
        ],
        scratch_shapes=[pltpu.VMEM((rows, width), bf16)],
    )(grad, mod, sub, qkv, probs, ctx, branch, *wo)


def spatial_input_kernel(grad, mod, x, dqkv, wi0, wi1, out, dmod):
    cols = wi0.shape[2]
    g = 0.0
    for h, w in enumerate((wi0, wi1)):
        for i in range(3):
            g = g + dot(dqkv[i, :, h * cols : (h + 1) * cols], w[i], NT)
    normed, inv_std = norm(x[...].astype(f32))
    dmod[0, 0:1] = column_sum(g)
    dmod[0, 1:2] = column_sum(g * normed)
    out[...] = grad[...] + norm_back(g, normed, inv_std, mod[0, 1:2])


def spatial_input(grad, mod, x, dqkv, wi):
    frames = mod.shape[0]
    rows, width = x.shape
    n = rows // frames
    tokens = pl.BlockSpec((n, width), lambda f: (f, 0))
    return call(
        spatial_input_kernel,
        6 * rows * width * width,
        6 * width * width + 16 * rows * width,
        grid=(frames,),
        in_specs=[
            tokens,
            pl.BlockSpec((1,) + mod.shape[1:], lambda f: (f, 0, 0)),
            tokens,
            pl.BlockSpec((3, n, width), lambda f: (0, f, 0)),
            whole(wi[0].shape),
            whole(wi[1].shape),
        ],
        out_specs=[tokens, pl.BlockSpec((1, 2, width), lambda f: (f, 0, 0))],
        out_shape=[shape((rows, width), f32), shape((frames, 2, width), f32)],
    )(grad, mod, x, dqkv, *wi)


def split_dot(x, b):
    hi = x.astype(bf16)
    return dot(hi, b) + dot((x - hi.astype(f32)).astype(bf16), b)


def head_maps(width):
    feature = lax.broadcasted_iota(jnp.int32, (width, LANES), 0) // HD
    head = lax.broadcasted_iota(jnp.int32, (width, LANES), 1)
    gather = (feature == head).astype(bf16)
    feature = lax.broadcasted_iota(jnp.int32, (LANES, width), 1) // HD
    head = lax.broadcasted_iota(jnp.int32, (LANES, width), 0)
    return gather, (feature == head).astype(bf16)


def temporal_kernel(
    x0, x1, b0, b1, mod, bias, wi0, wi1, wo0, wo1, stream, stream2, sub, qkv, probs, ctx, branch
):
    width, cols, frames = sub.shape[1], wi0.shape[2], mod.shape[0]
    n = sub.shape[0] // frames
    at = [pl.ds(f * n, n) for f in range(frames)]
    for f in range(frames):
        xs, bs = (x0, b0) if f < frames // 2 else (x1, b1)
        source = at[f % (frames // 2)]
        s = xs[source, :].astype(f32) + mod[f, 0:1] * bs[source, :].astype(f32)
        stream[at[f], :] = s
        normed, _ = norm(s)
        sub[at[f], :] = (normed * mod[f, 2:3] + mod[f, 1:2]).astype(bf16)
    project(sub[...], (wi0, wi1), qkv)
    gather, spread = head_maps(width)
    for f in range(frames):
        q = qkv[0, at[f], :].astype(f32)
        scores = [
            split_dot(q * qkv[1, at[g], :].astype(f32), gather) + bias[f, g] for g in range(frames)
        ]
        top = functools.reduce(jnp.maximum, scores)
        e = [jnp.exp(s - top) for s in scores]
        inv = 1.0 / sum(e)
        context = 0.0
        for g in range(frames):
            p = (e[g] * inv).astype(bf16)
            probs[f * frames + g] = p
            context = context + dot(p, spread) * qkv[2, at[g], :].astype(f32)
        ctx[at[f], :] = context.astype(bf16)
    for f in range(frames):
        b = dot(ctx[at[f], :cols], wo0[...]) + dot(ctx[at[f], cols:], wo1[...])
        branch[at[f], :] = b.astype(bf16)
        stream2[at[f], :] = stream[at[f], :] + mod[f, 3:4] * b


def temporal(x0, x1, b0, b1, mod, bias, wi, wo):
    width, frames = x0.shape[1], mod.shape[0]
    rows = 2 * x0.shape[0]
    return call(
        temporal_kernel,
        8 * rows * width * width,
        8 * width * width + 30 * rows * width,
        16 * frames * rows,
        in_specs=[VM] * 5 + [SM] + [VM] * 4,
        out_specs=[VM] * 7,
        out_shape=[
            shape((rows, width), f32),
            shape((rows, width), f32),
            shape((rows, width), bf16),
            shape((3, rows, width), bf16),
            shape((frames * frames, rows // frames, LANES), bf16),
            shape((rows, width), bf16),
            shape((rows, width), bf16),
        ],
    )(x0, x1, b0, b1, mod, bias, *wi, *wo)


def temporal_back_kernel(
    grad, cot, mod, stream, sub, qkv, probs, ctx, branch, wi0, wi1, wo0, wo1,
    grad_own, delta_other, own, other, dmod, rows, dqkv,
):
    width, cols, frames = sub.shape[1], wo0.shape[0], mod.shape[0]
    n = sub.shape[0] // frames
    at = [pl.ds(f * n, n) for f in range(frames)]
    gather, spread = head_maps(width)
    context_grad = []
    for f in range(frames):
        g = grad[at[f], :]
        dmod[f, 2:3] = column_sum(g * branch[at[f], :].astype(f32)) * mod[f, 4:5]
        r = (g * mod[f, 3:4]).astype(bf16)
        rows[at[f], :] = r
        context_grad.append(
            jnp.concatenate([dot(r, wo0[...], NT), dot(r, wo1[...], NT)], axis=1).astype(bf16)
        )
    dk, dv = [0.0] * frames, [0.0] * frames
    for f in range(frames):
        d = context_grad[f].astype(f32)
        prob_grad = [split_dot(d * qkv[2, at[g], :].astype(f32), gather) for g in range(frames)]
        p = [probs[f * frames + g] for g in range(frames)]
        p32 = [a.astype(f32) for a in p]
        total = sum(a * b for a, b in zip(prob_grad, p32))
        q = qkv[0, at[f], :].astype(f32)
        dq = 0.0
        for g in range(frames):
            ds = dot((p32[g] * (prob_grad[g] - total)).astype(bf16), spread)
            dq = dq + ds * qkv[1, at[g], :].astype(f32)
            dk[g] = dk[g] + ds * q
            dv[g] = dv[g] + dot(p[g], spread) * d
        dqkv[0, at[f], :] = (dq * SCALE).astype(bf16)
    for g in range(frames):
        dqkv[1, at[g], :] = dk[g].astype(bf16)
        dqkv[2, at[g], :] = dv[g].astype(bf16)
    for h, out in ((1, other), (0, own)):
        half = slice(h * cols, (h + 1) * cols)
        for i in range(3):
            out[:, i * cols : (i + 1) * cols] = dot(sub[...], dqkv[i, :, half], TN).astype(bf16)
        out[:, 3 * cols :] = dot(rows[...], ctx[:, half], TN).astype(bf16)
    for f in range(frames):
        g = 0.0
        for h, w in enumerate((wi0, wi1)):
            for i in range(3):
                g = g + dot(dqkv[i, at[f], h * cols : (h + 1) * cols], w[i], NT)
        normed, inv_std = norm(stream[at[f], :])
        dmod[f, 0:1] = column_sum(g)
        dmod[f, 1:2] = column_sum(g * normed)
        new = grad[at[f], :] + norm_back(g, normed, inv_std, mod[f, 2:3])
        if f < frames // 2:
            grad_own[at[f], :] = new
        else:
            delta_other[at[f - frames // 2], :] = (new - cot[at[f], :].astype(f32)).astype(bf16)


def temporal_back(grad, cot, mod, stream, sub, qkv, probs, ctx, branch, wi, wo):
    rows, width = sub.shape
    frames, cols = mod.shape[0], wo[0].shape[0]
    return call(
        temporal_back_kernel,
        16 * rows * width * width,
        16 * width * width + 40 * rows * width,
        in_specs=[VM] * 13,
        out_specs=[VM] * 5,
        out_shape=[
            shape((rows // 2, width), f32),
            shape((rows // 2, width), bf16),
            shape((width, 4 * cols), bf16),
            shape((width, 4 * cols), bf16),
            shape((frames, 3, width), f32),
        ],
        scratch_shapes=[pltpu.VMEM((rows, width), bf16), pltpu.VMEM((3, rows, width), bf16)],
    )(grad, cot, mod, stream, sub, qkv, probs, ctx, branch, *wi, *wo)


def gelu_both(u):
    k = 0.7978845608028654
    squared = u * u
    th = jnp.tanh(u * (k + (k * 0.044715) * squared))
    half = 0.5 * (1.0 + th)
    return u * half, half + (0.5 * u) * (1.0 - th * th) * (k + (3 * k * 0.044715) * squared)


def feed_kernel(last, frames, *refs):
    refs = list(refs)
    stream, cot, mod, wu, wd = refs[:5]
    if last:
        sub, rows, branch_in, input_in, branch, inputs, grads, out, grad_out, dmod = refs[5:]
    else:
        sub, rows, branch, inputs, grads = refs[5:]
    step, steps = pl.program_id(0), pl.num_programs(0)
    n = stream.shape[0] // frames

    @pl.when(step == 0)
    def _():
        if last:
            branch[...] = branch_in[...]
            inputs[...] = input_in[...]
            return
        for f in range(frames):
            at = pl.ds(f * n, n)
            normed, _ = norm(stream[at, :])
            sub[at, :] = (normed * mod[1, f : f + 1] + mod[0, f : f + 1]).astype(bf16)
            rows[at, :] = (mod[2, f : f + 1] * cot[at, :].astype(f32)).astype(bf16)
        branch[...] = jnp.zeros_like(branch)
        inputs[...] = jnp.zeros_like(inputs)

    act, slope = gelu_both(dot(sub[...], wu[...]))
    act = act.astype(bf16)
    pre_grad = (slope * dot(rows[...], wd[...], NT)).astype(bf16)
    branch[...] += dot(act, wd[...])
    inputs[...] += dot(pre_grad, wu[...], NT)
    grads[0] = dot(sub[...], pre_grad, TN).astype(bf16)
    grads[1] = dot(rows[...], act, TN).astype(bf16)
    if not last:
        return

    @pl.when(step == steps - 1)
    def _():
        for f in range(frames):
            at = pl.ds(f * n, n)
            s, g, b, d = stream[at, :], cot[at, :].astype(f32), branch[at, :], inputs[at, :]
            normed, inv_std = norm(s)
            out[at, :] = (s + mod[2, f : f + 1] * b).astype(bf16)
            dmod[0, f : f + 1] = column_sum(d)
            dmod[1, f : f + 1] = column_sum(d * normed)
            dmod[2, f : f + 1] = column_sum(b * g) * mod[3, f : f + 1]
            grad_out[at, :] = g + norm_back(d, normed, inv_std, mod[1, f : f + 1])


def feed(last, stream, cot, mod, wu, wd, state=()):
    rows, width = stream.shape
    hidden, frames = wu.shape[1], mod.shape[1]
    chunk = 512
    tokens = whole((rows, width))
    out_specs = [tokens, tokens]
    out_shape = [shape((rows, width), f32)] * 2
    if not last:
        out_specs = [tokens, tokens] + out_specs
        out_shape = [shape((rows, width), bf16)] * 2 + out_shape
    out_specs.append(pl.BlockSpec((2, width, chunk), lambda i: (0, 0, i)))
    out_shape.append(shape((2, width, hidden), bf16))
    if last:
        out_specs += [tokens, tokens, whole((3, frames, width))]
        out_shape += [
            shape((rows, width), bf16),
            shape((rows, width), f32),
            shape((3, frames, width), f32),
        ]
    return call(
        functools.partial(feed_kernel, last, frames),
        12 * rows * width * hidden,
        10 * rows * width + 8 * width * hidden,
        rows * hidden,
        grid=(hidden // chunk,),
        in_specs=[
            tokens,
            tokens,
            whole(mod.shape),
            pl.BlockSpec((width, chunk), lambda i: (0, i)),
            pl.BlockSpec((chunk, width), lambda i: (i, 0)),
        ]
        + [tokens] * len(state),
        out_specs=out_specs,
        out_shape=out_shape,
    )(stream, cot, mod, wu, wd, *state)


def local(
    patches_in, cotangent, condition, frame_clip, frame_valid, w_ada, sp_qkv, sp_out, tm_qkv, tm_out, w_up, w_down,
    dp_size,
):
    frames, patches, width = patches_in.shape
    half = patches // 2
    clips = condition.shape[0]
    t = lax.axis_index("tensor")
    d = lax.axis_index("dp")
    first = t == 0

    def swap(a):
        return lax.ppermute(a, "tensor", [(0, 1), (1, 0)])

    def rows_of(a):
        return a.reshape(-1, width)

    def to_patch_split(a):
        own = lax.dynamic_slice_in_dim(a, t * half, half, 1)
        other = lax.dynamic_slice_in_dim(a, (1 - t) * half, half, 1)
        return rows_of(own), swap(rows_of(other))

    def to_frame_split(own, received):
        own, received = (a.reshape(frames, half, width) for a in (own, received))
        return jnp.where(
            first, jnp.concatenate([own, received], axis=1), jnp.concatenate([received, own], axis=1)
        )

    def own_first(a):
        return jnp.where(first, a, jnp.concatenate([a[frames:], a[:frames]], axis=0))

    sq, so, tq, to, up, dn = (
        (w, swap(w)) for w in (sp_qkv, sp_out, tm_qkv, tm_out, w_up, w_down)
    )
    clip_ids = own_first(frame_clip)
    valid_ids = own_first(frame_valid)
    onehot = (clip_ids[:, None] == jnp.arange(clips, dtype=jnp.int32)[None, :]).astype(f32)
    cond_rows = jnp.dot(onehot, condition, precision=highest)
    act_low = jax.nn.silu(cond_rows).astype(bf16)
    mods = jnp.dot(act_low, w_ada, preferred_element_type=f32).reshape(2 * frames, 9, width)
    valid = jnp.broadcast_to(valid_ids.astype(f32)[:, None], (2 * frames, width))
    shift = [mods[:, 3 * b] for b in range(3)]
    scale1 = [1.0 + mods[:, 3 * b + 1] for b in range(3)]
    gate = [valid * mods[:, 3 * b + 2] for b in range(3)]
    mod0 = jnp.stack([shift[0], scale1[0], gate[0], valid], axis=1)[:frames]
    mod1 = jnp.stack([gate[0], shift[1], scale1[1], gate[1], valid], axis=1)
    mod2 = jnp.stack([shift[2], scale1[2], gate[2], valid], axis=0)
    allowed = (clip_ids[:, None] == clip_ids[None, :]) & (valid_ids[None, :] == 1) | jnp.eye(
        2 * frames, dtype=bool
    )
    bias = jnp.where(allowed, 0.0, -1e30)
    x_split = to_patch_split(patches_in)
    c_split = jnp.concatenate(to_patch_split(cotangent), axis=0)
    x = rows_of(patches_in)

    sub0, qkv0, probs0, ctx0, branch0 = spatial(x, mod0, sq, so)
    b_split = to_patch_split(branch0.reshape(patches_in.shape))
    stream1, stream2, sub1, qkv1, probs1, ctx1, branch1 = temporal(
        *x_split, *b_split, mod1, bias, tq, to
    )
    *state, feed_other = feed(False, stream2, c_split, mod2, up[1], dn[1])
    _, _, feed_own, out_split, grad, dmod2 = feed(True, stream2, c_split, mod2, up[0], dn[0], state)
    own_rows = frames * half
    patches_out = to_frame_split(out_split[:own_rows], swap(out_split[own_rows:]))
    grad_own, delta, tm_own, tm_other, dmod1 = temporal_back(
        grad, c_split, mod1, stream1, sub1, qkv1, probs1, ctx1, branch1, tq, to
    )
    other_cot = lax.dynamic_slice_in_dim(cotangent, (1 - t) * half, half, 1)
    grad_other = rows_of(other_cot).astype(f32) + swap(delta).astype(f32)
    grad = rows_of(to_frame_split(grad_own, grad_other))
    dqkv, sp_own, sp_other, dgate0 = spatial_back(
        grad, mod0, sub0, qkv0, probs0, ctx0, branch0, so
    )
    grad, dmod0 = spatial_input(grad, mod0, x, dqkv, sq)

    bit0, bit1, rest = d % 2, d // 2 % 2, d // 4
    outer = dp_size // 4

    def both_cores(first_bit, second_bit):
        return [(2 * i, 2 * (i ^ first_bit)) for i in range(dp_size)] + [
            (2 * i + 1, 2 * (i ^ second_bit) + 1) for i in range(dp_size)
        ]

    def pick(a, axis, at):
        return lax.dynamic_index_in_dim(a, at, axis, keepdims=False)

    def reduce_dp(own, other):
        total = (own.astype(f32) + swap(other).astype(f32)).astype(bf16)
        columns = total.shape[-1]
        a = total.reshape(-1, outer, 2, 2, width // dp_size, columns)
        keep = jnp.where(first, pick(a, 3, bit0), pick(a, 2, bit1))
        send = jnp.where(first, pick(a, 3, 1 - bit0), pick(a, 2, 1 - bit1))
        b = keep + lax.ppermute(send, ("dp", "tensor"), both_cores(1, 2))
        bit = jnp.where(first, bit1, bit0)
        keep, send = pick(b, 2, bit), pick(b, 2, 1 - bit)
        c = keep + lax.ppermute(send, ("dp", "tensor"), both_cores(2, 1))
        if outer != 4:
            groups = [[4 * z + i for z in range(outer)] for i in range(4)]
            return lax.psum_scatter(
                c.astype(f32), "dp", scatter_dimension=1, axis_index_groups=groups, tiled=False
            )
        total = pick(c, 1, rest).astype(f32)
        for k in range(1, outer):
            piece = pick(c, 1, (rest + k) % outer)
            total = total + lax.ppermute(
                piece, "dp", [(i, (i + 4 * k) % dp_size) for i in range(dp_size)]
            ).astype(f32)
        return total

    up_out, down_out = reduce_dp(feed_own, feed_other)
    tm_sum = reduce_dp(tm_own, tm_other)[0]
    sp_sum = reduce_dp(sp_own, sp_other)[0]

    def attention_grads(a):
        a = a.reshape(a.shape[0], 4, -1).transpose(1, 0, 2)
        return a[:3], a[3].T

    shared = jnp.concatenate(
        [dmod1.reshape(2 * frames, -1), dmod2.transpose(1, 0, 2).reshape(2 * frames, -1)], axis=1
    )
    late = jnp.concatenate([dmod0, dgate0], axis=1).reshape(frames, -1)
    mine = jnp.concatenate([late, shared[:frames] + swap(shared[frames:])], axis=1)
    hi = mine.astype(bf16)
    mid = (mine - hi.astype(f32)).astype(bf16)
    low = (mine - hi.astype(f32) - mid.astype(f32)).astype(bf16)
    parts = jnp.concatenate([hi, mid, low], axis=0)
    act_grad = lax.dot_general(parts, w_ada, (((1,), (1,)), ((), ())), preferred_element_type=f32)
    act_grad = act_grad[:frames] + act_grad[frames : 2 * frames] + act_grad[2 * frames :]
    unused, silu_back = jax.vjp(jax.nn.silu, cond_rows[:frames])
    cond_term = silu_back(act_grad)[0]
    devices = 2 * dp_size
    own_ids = clip_ids[:frames].astype(f32)
    payload = jnp.concatenate(
        [
            mine.reshape(frames, devices, -1),
            cond_term.reshape(frames, devices, -1),
            jnp.broadcast_to(own_ids[:, None, None], (frames, devices, 1)),
        ],
        axis=2,
    )
    got = lax.all_to_all(
        payload.transpose(1, 0, 2), ("dp", "tensor"), split_axis=0, concat_axis=0, tiled=True
    ).reshape(devices * frames, -1)
    ada_cols = 9 * width // devices
    ids = got[:, -1].astype(jnp.int32)
    every = (ids[:, None] == jnp.arange(clips, dtype=jnp.int32)[None, :]).astype(f32)
    act_all = jnp.dot(
        every, jax.nn.silu(condition).astype(bf16).astype(f32), precision=highest
    )
    ada_grad = jnp.dot(act_all.T, got[:, :ada_cols], precision=highest)
    condition_grad = jnp.dot(every.T, got[:, ada_cols:-1], precision=highest)
    return (
        patches_out.reshape(patches_in.shape),
        grad.reshape(patches_in.shape),
        condition_grad,
        ada_grad,
        *attention_grads(sp_sum),
        *attention_grads(tm_sum),
        up_out,
        down_out.T,
    )


def solution(mesh):
    return jax.shard_map(
        functools.partial(local, dp_size=mesh.shape["dp"]),
        mesh=mesh,
        in_specs=(
            P(("dp", "tensor"), None, None),
            P(("dp", "tensor"), None, None),
            P(),
            P("dp"),
            P("dp"),
            P(),
            P(None, None, "tensor"),
            P("tensor", None),
            P(None, None, "tensor"),
            P("tensor", None),
            P(None, "tensor"),
            P("tensor", None),
        ),
        out_specs=(
            P(("dp", "tensor"), None, None),
            P(("dp", "tensor"), None, None),
            P(None, ("dp", "tensor")),
            P(None, ("dp", "tensor")),
            P(None, "dp", "tensor"),
            P("tensor", "dp"),
            P(None, "dp", "tensor"),
            P("tensor", "dp"),
            P("dp", "tensor"),
            P("tensor", "dp"),
        ),
        check_vma=False,
    )
```

```python
import functools
import math

import jax
import jax.numpy as jnp
from jax import lax
from jax.experimental import pallas as pl
from jax.experimental.pallas import tpu as pltpu
from jax.sharding import PartitionSpec as P

HD = 64
LANES = 128
SCALE = HD**-0.5
f32 = jnp.float32
bf16 = jnp.bfloat16
highest = lax.Precision.HIGHEST
epsilon = 1e-06
ROOM = 12 * 2**20
PIECES = 6
NN = (((1,), (0,)), ((), ()))
NT = (((1,), (1,)), ((), ()))
TN = (((0,), (0,)), ((), ()))
VM = pl.BlockSpec(memory_space=pltpu.VMEM)
SM = pl.BlockSpec(memory_space=pltpu.SMEM)
shape = jax.ShapeDtypeStruct


def dot(a, b, dims=NN):
    return lax.dot_general(a, b, dims, preferred_element_type=f32)


def norm(x):
    centred = x - jnp.mean(x, -1, keepdims=True)
    inv_std = lax.rsqrt(jnp.mean(centred * centred, -1, keepdims=True) + epsilon)
    return centred * inv_std, inv_std


def norm_back(input_grad, normed, inv_std, scale1):
    d = input_grad * scale1
    return inv_std * (
        d - jnp.mean(d, -1, keepdims=True) - normed * jnp.mean(d * normed, -1, keepdims=True)
    )


def column_sum(x):
    return jnp.sum(x, 0, keepdims=True)


def whole(dims):
    return pl.BlockSpec(dims, lambda *at: (0,) * len(dims))


def call(kernel, flops, bytes_accessed, limit, exps=0, **options):
    return pl.pallas_call(
        kernel,
        compiler_params=pltpu.CompilerParams(vmem_limit_bytes=limit),
        cost_estimate=pl.CostEstimate(
            flops=flops // 100, bytes_accessed=bytes_accessed // 100, transcendentals=exps // 100
        ),
        **options,
    )


def in_hbm(a):
    return pltpu.with_memory_space_constraint(a, pltpu.HBM)


def size_of(a):
    return math.prod(a.shape) * jnp.dtype(a.dtype).itemsize


class Far:
    def __init__(self, array):
        self.array = array


def staged(body, small, ins, outs, scratch, flops, exps=0):
    ns, ni, no = len(small), len(ins), len(outs)
    far_i = [i for i in range(ni) if isinstance(ins[i], Far)]
    far_o = [i for i in range(no) if isinstance(outs[i], Far)]
    ins = [a.array if isinstance(a, Far) else a for a in ins]
    outs = [a.array if isinstance(a, Far) else a for a in outs]

    def kernel(*refs):
        few, refs = refs[:ns], refs[ns:]
        in_refs, out_refs, refs = list(refs[:ni]), list(refs[ni : ni + no]), refs[ni + no :]
        near_i, near_o = refs[: len(far_i)], refs[len(far_i) : len(far_i) + len(far_o)]
        rest, in_sems, out_sems = refs[len(far_i) + len(far_o) : -2], refs[-2], refs[-1]
        copies, results, started = {}, {}, []
        for k, i in enumerate(far_i):
            copies[i] = pltpu.make_async_copy(in_refs[i], near_i[k], in_sems.at[k])
            copies[i].start()
            in_refs[i] = near_i[k]
        for k, i in enumerate(far_o):
            results[i] = (near_o[k], out_refs[i])
            out_refs[i] = near_o[k]

        def need(*which):
            for i in which:
                if i in copies:
                    copies[i].wait()

        def done(*which, at=slice(None)):
            for i in which:
                if i in results:
                    source, target = (r.at[at] for r in results[i])
                    copy = pltpu.make_async_copy(source, target, out_sems.at[len(started)])
                    copy.start()
                    started.append(copy)

        body(need, done, *few, *in_refs, *out_refs, *rest)
        for c in started:
            c.wait()

    far = pl.BlockSpec(memory_space=pltpu.HBM)
    kept = [pltpu.VMEM(ins[i].shape, ins[i].dtype) for i in far_i]
    kept += [pltpu.VMEM(outs[i].shape, outs[i].dtype) for i in far_o]
    own = [a for a in scratch if hasattr(a, "shape")]
    return call(
        kernel,
        flops,
        sum(size_of(a) for a in (*ins, *outs)),
        ROOM + sum(size_of(a) for a in (*kept, *own)),
        exps,
        in_specs=[SM] * ns + [far if i in far_i else VM for i in range(ni)],
        out_specs=[far if i in far_o else VM for i in range(no)],
        out_shape=[
            pltpu.HBM(a.shape, a.dtype) if i in far_o else a for i, a in enumerate(outs)
        ],
        scratch_shapes=kept
        + scratch
        + [
            pltpu.SemaphoreType.DMA((max(1, len(far_i)),)),
            pltpu.SemaphoreType.DMA((PIECES * max(1, len(far_o)),)),
        ],
    )(*small, *(in_hbm(a) if i in far_i else a for i, a in enumerate(ins)))


def head_masks():
    lane = lax.broadcasted_iota(jnp.int32, (1, LANES), 1)
    return [(lane < HD).astype(bf16), (lane >= HD).astype(bf16)]


class Mods:
    def __init__(self, mods, valid, f, b, width):
        def row(i):
            return mods[pl.ds(f, 1), (3 * b + i) * width : (3 * b + i + 1) * width]

        self.shift, self.scale1 = row(0), 1.0 + row(1)
        self.valid = valid[f]
        self.gate = row(2) * self.valid


def project(sub, weights, qkv, rows=slice(None)):
    cols = weights[0].shape[2]
    for h, w in enumerate(weights):
        for i in range(3):
            y = dot(sub, w[i])
            if i == 0:
                y = y * SCALE
            qkv[i, rows, h * cols : (h + 1) * cols] = y.astype(bf16)


def input_sum(dqkv, weights, rows=slice(None)):
    cols, g = weights[0].shape[2], 0.0
    for d, w in zip(dqkv, weights):
        for i in range(3):
            g = g + dot(d[rows, i * cols : (i + 1) * cols], w[i], NT)
    return g


def spatial_kernel(
    need, done, side, valid, x, mods, wi0, wi1, wo0, wo1, sub, qkv, probs, ctx0, ctx1, branch, near, far
):
    frames = valid.shape[0] // 2
    n, width = x.shape[0] // frames, x.shape[1]
    cols, half = wi0.shape[2], n // 2
    masks = head_masks()
    need(0, 1)
    for f in range(frames):
        here = slice(f * n, (f + 1) * n)
        m = Mods(mods, valid, f, 0, width)
        normed, _ = norm(x[here, :].astype(f32))
        sub[here, :] = (normed * m.scale1 + m.shift).astype(bf16)
    done(0)
    for f in range(frames):
        here = slice(f * n, (f + 1) * n)
        if f == 0:
            need(2, 3)
        project(sub[here, :], (wi0, wi1), qkv, here)
        for h, ctx in enumerate((ctx0, ctx1)):
            for j in range(cols // LANES):
                low = slice(j * LANES, (j + 1) * LANES)
                at = slice(h * cols + j * LANES, h * cols + (j + 1) * LANES)
                q, k, v = qkv[0, here, at], qkv[1, here, at], qkv[2, here, at]
                out = 0.0
                for a in range(2):
                    scores = dot(q * masks[a], k, NT)
                    e = jnp.exp(scores - jnp.max(scores, -1, keepdims=True))
                    p = (e * (1.0 / jnp.sum(e, -1, keepdims=True))).astype(bf16)
                    probs[f * (width // HD) + h * (cols // HD) + 2 * j + a] = p
                    out = out + dot(p, v * masks[a])
                ctx[here, low] = out.astype(bf16)
        heads = width // HD
        done(2, at=pl.ds(f * heads, heads))
        done(3, 4, at=pl.ds(f * n, n))
        if f == frames - 1:
            done(1)
        if f == 0:
            need(4, 5)
        y = dot(ctx0[here, :], wo0[...]) + dot(ctx1[here, :], wo1[...])
        branch[here, :] = y.astype(bf16)
        to = slice(f * half, (f + 1) * half)
        near[to, :] = branch[pl.ds(pl.multiple_of(f * n + side[0] * half, half), half), :]
        far[to, :] = branch[pl.ds(pl.multiple_of(f * n + (1 - side[0]) * half, half), half), :]
    done(5)


def spatial(side, valid, x, mods, wi, wo):
    rows, width = x.shape
    frames, heads, cols = valid.shape[0] // 2, width // HD, wo[0].shape[0]
    n = rows // frames
    return staged(
        spatial_kernel,
        [side, valid],
        [Far(x), mods, *(Far(w) for w in (*wi, *wo))],
        [
            Far(shape((rows, width), bf16)),
            Far(shape((3, rows, width), bf16)),
            Far(shape((frames * heads, n, n), bf16)),
            Far(shape((rows, cols), bf16)),
            Far(shape((rows, cols), bf16)),
            Far(shape((rows, width), bf16)),
            shape((rows // 2, width), bf16),
            shape((rows // 2, width), bf16),
        ],
        [],
        rows * width * (8 * width + 4 * n),
        frames * heads * n * n,
    )


def spatial_back_kernel(
    need, done, side, valid, near, far, cot, mods, qkv, probs, ctx0, ctx1, branch, wo0, wo1,
    grad, rows, dqkv0, dqkv1, dgate,
):
    frames = valid.shape[0] // 2
    n, width = cot.shape[0] // frames, cot.shape[1]
    cols, half = wo0.shape[0], n // 2
    masks = head_masks()
    need(0, 1, 2, 3, 8, 9, 10)
    for f in range(frames):
        all_rows = slice(f * n, (f + 1) * n)
        m = Mods(mods, valid, f, 0, width)
        source = slice(f * half, (f + 1) * half)
        here = pl.ds(pl.multiple_of(f * n + side[0] * half, half), half)
        there = pl.ds(pl.multiple_of(f * n + (1 - side[0]) * half, half), half)
        grad[here, :] = near[source, :]
        grad[there, :] = cot[there, :].astype(f32) + far[source, :].astype(f32)
        g = grad[all_rows, :]
        dgate[f : f + 1, :] = column_sum(g * branch[all_rows, :].astype(f32)) * m.valid
        rows[all_rows, :] = (g * m.gate).astype(bf16)
    context_grads = [dot(rows[...], w[...], NT).astype(bf16) for w in (wo0, wo1)]
    need(4, 5, 6, 7)
    for f in range(frames):
        all_rows = slice(f * n, (f + 1) * n)
        for h, (ctx, dqkv) in enumerate(((ctx0, dqkv0), (ctx1, dqkv1))):
            for j in range(cols // LANES):
                low = slice(j * LANES, (j + 1) * LANES)
                at = slice(h * cols + j * LANES, h * cols + (j + 1) * LANES)
                q, k, v = qkv[0, all_rows, at], qkv[1, all_rows, at], qkv[2, all_rows, at]
                d = context_grads[h][all_rows, low]
                product = d.astype(f32) * ctx[all_rows, low].astype(f32)
                dq = dk = dv = 0.0
                for a in range(2):
                    da = d * masks[a]
                    p = probs[f * (width // HD) + h * (cols // HD) + 2 * j + a]
                    delta = jnp.sum(product * masks[a].astype(f32), -1, keepdims=True)
                    ds = (p.astype(f32) * (dot(da, v, NT) - delta)).astype(bf16)
                    dv = dv + dot(p, da, TN)
                    dq = dq + dot(ds, k * masks[a])
                    dk = dk + dot(ds, q * masks[a], TN)
                for i, y in enumerate((dq * SCALE, dk, dv)):
                    to = i * cols + j * LANES
                    dqkv[all_rows, to : to + LANES] = y.astype(bf16)


def spatial_back(side, valid, near, far, cot, mods, qkv, probs, ctx, branch, wo):
    rows, width = cot.shape
    frames, cols = valid.shape[0] // 2, wo[0].shape[0]
    n = rows // frames
    return staged(
        spatial_back_kernel,
        [side, valid],
        [near, far, Far(cot), mods, *(Far(a) for a in (qkv, probs, *ctx, branch, *wo))],
        [
            shape((rows, width), f32),
            shape((rows, width), bf16),
            shape((rows, 3 * cols), bf16),
            shape((rows, 3 * cols), bf16),
            shape((frames, width), f32),
        ],
        [],
        rows * width * (2 * width + 10 * n),
    )


def spatial_input_kernel(
    need, done, side, valid, grad, mods, x, near, far, dqkv0, dqkv1, wi0, wi1, out, layer_out, dmod
):
    frames = valid.shape[0] // 2
    n, width = x.shape[0] // frames, x.shape[1]
    half = n // 2
    need(7, 8)
    inputs = input_sum((dqkv0, dqkv1), (wi0, wi1))
    need(0, 1, 2, 3, 4, 5, 6)
    for f in range(frames):
        m = Mods(mods, valid, f, 0, width)
        here = pl.ds(pl.multiple_of(f * n + side[0] * half, half), half)
        there = pl.ds(pl.multiple_of(f * n + (1 - side[0]) * half, half), half)
        layer_out[here, :] = near[f * half : (f + 1) * half, :]
        layer_out[there, :] = far[f * half : (f + 1) * half, :]
        at = slice(f * n, (f + 1) * n)
        g = inputs[at]
        normed, inv_std = norm(x[at, :].astype(f32))
        dmod[f : f + 1, :width] = column_sum(g)
        dmod[f : f + 1, width:] = column_sum(g * normed)
        out[at, :] = grad[at, :] + norm_back(g, normed, inv_std, m.scale1)
    done(0, 1, 2)


def spatial_input(side, valid, grad, mods, x, near, far, dqkv, wi):
    rows, width = x.shape
    return staged(
        spatial_input_kernel,
        [side, valid],
        [grad, mods, Far(x), Far(near), Far(far), *dqkv, *(Far(w) for w in wi)],
        [
            Far(shape((rows, width), f32)),
            Far(shape((rows, width), bf16)),
            shape((valid.shape[0] // 2, 2 * width), f32),
        ],
        [],
        6 * rows * width * width,
    )


BLOCKS = 16


def store_ordered(order, scratch, keep, send, columns):
    size = scratch.shape[0] // BLOCKS
    for p in range(BLOCKS):
        out = keep if p < BLOCKS // 2 else send
        to = (p % (BLOCKS // 2)) * size
        at = pl.ds(pl.multiple_of(order[p] * size, size), size)
        out[to : to + size, columns] = scratch[at, :]


def weights_kernel(need, done, order, s0, d0, s1, d1, r0, c0, r1, c1, keep, send, wide, narrow):
    split = d0.shape[1]
    need(0, 1)
    total = dot(s0[...], d0[...], TN)
    need(2, 3)
    wide[...] = (total + dot(s1[...], d1[...], TN)).astype(bf16)
    store_ordered(order, wide, keep, send, slice(0, split))
    need(4, 5, 6, 7)
    narrow[...] = (dot(r0[...], c0[...], TN) + dot(r1[...], c1[...], TN)).astype(bf16)
    store_ordered(order, narrow, keep, send, slice(split, keep.shape[1]))
    done(0, 1)


def weights(order, sub, dqkv, rows, ctx):
    n, width = sub[0].shape
    split, cols = dqkv[0].shape[1], ctx[0].shape[1]
    return staged(
        weights_kernel,
        [order],
        [Far(sub[0]), dqkv[0], Far(sub[1]), dqkv[1], rows[0], Far(ctx[0]), rows[1], Far(ctx[1])],
        [shape((width // 2, split + cols), bf16)] * 2,
        [pltpu.VMEM((width, split), bf16), pltpu.VMEM((width, cols), bf16)],
        4 * n * width * (split + cols),
    )


def head_sums(products, gather, stack):
    n, count = products[0].shape[0], len(products)
    for i, x in enumerate(products):
        hi = x.astype(bf16)
        stack[i * n : (i + 1) * n, :] = hi
        stack[(count + i) * n : (count + i + 1) * n, :] = (x - hi.astype(f32)).astype(bf16)
    y = dot(stack[...], gather)
    return [y[i * n : (i + 1) * n] + y[(count + i) * n : (count + i + 1) * n] for i in range(count)]


def head_maps(width):
    feature = lax.broadcasted_iota(jnp.int32, (width, LANES), 0) // HD
    head = lax.broadcasted_iota(jnp.int32, (width, LANES), 1)
    gather = (feature == head).astype(bf16)
    feature = lax.broadcasted_iota(jnp.int32, (LANES, width), 1) // HD
    head = lax.broadcasted_iota(jnp.int32, (LANES, width), 0)
    return gather, (feature == head).astype(bf16)


def temporal_kernel(
    need, done, side, valid, bias, x0, x1, b0, b1, mods, wi0, wi1, wo0, wo1,
    stream, sub, qkv, probs, ctx0, ctx1, branch, stream2, sub2, stack, small,
):
    rows, width = sub.shape
    cols, frames = wi0.shape[2], mods.shape[0]
    n = rows // frames
    at = [pl.ds(f * n, n) for f in range(frames)]
    need(0, 1, 2, 3, 4)
    for f in range(frames):
        xs, bs = (x0, b0) if f < frames // 2 else (x1, b1)
        g = f % (frames // 2)
        source = pl.ds(pl.multiple_of((2 * g + side[0]) * n, n), n)
        before, m = Mods(mods, valid, f, 0, width), Mods(mods, valid, f, 1, width)
        s = xs[source, :].astype(f32) + before.gate * bs[at[g], :].astype(f32)
        stream[at[f], :] = s
        normed, _ = norm(s)
        sub[at[f], :] = (normed * m.scale1 + m.shift).astype(bf16)
    done(0, 1)
    need(5, 6)
    project(sub[...], (wi0, wi1), qkv)
    done(2)
    gather, spread = head_maps(width)
    for f in range(frames):
        q = qkv[0, at[f], :].astype(f32)
        scores = head_sums(
            [q * qkv[1, at[g], :].astype(f32) for g in range(frames)], gather, stack
        )
        scores = [s + bias[f, g] for g, s in enumerate(scores)]
        top = functools.reduce(jnp.maximum, scores)
        e = [jnp.exp(s - top) for s in scores]
        inv = 1.0 / sum(e)
        for g in range(frames):
            p = (e[g] * inv).astype(bf16)
            probs[f * frames + g] = p
            small[at[g], :] = p
        spread_p = dot(small[...], spread)
        context = sum(
            spread_p[g * n : (g + 1) * n] * qkv[2, at[g], :].astype(f32) for g in range(frames)
        )
        ctx0[at[f], :] = context[:, :cols].astype(bf16)
        ctx1[at[f], :] = context[:, cols:].astype(bf16)
    done(3, 4, 5)
    need(7, 8)
    for f in range(frames):
        m, after = Mods(mods, valid, f, 1, width), Mods(mods, valid, f, 2, width)
        b = dot(ctx0[at[f], :], wo0[...]) + dot(ctx1[at[f], :], wo1[...])
        branch[at[f], :] = b.astype(bf16)
        s = stream[at[f], :] + m.gate * b
        stream2[at[f], :] = s
        normed, _ = norm(s)
        sub2[at[f], :] = (normed * after.scale1 + after.shift).astype(bf16)
    done(6, 7, 8)


def temporal(side, valid, bias, x0, x1, b0, b1, mods, wi, wo):
    rows, width = x0.shape
    frames, cols = mods.shape[0], wo[0].shape[0]
    n = rows // frames
    return staged(
        temporal_kernel,
        [side, valid, bias],
        [Far(x0), Far(x1), b0, b1, mods, *(Far(w) for w in (*wi, *wo))],
        [
            Far(shape((rows, width), f32)),
            Far(shape((rows, width), bf16)),
            Far(shape((3, rows, width), bf16)),
            Far(shape((frames * frames, n, LANES), bf16)),
            Far(shape((rows, cols), bf16)),
            Far(shape((rows, cols), bf16)),
            Far(shape((rows, width), bf16)),
            Far(shape((rows, width), f32)),
            shape((rows, width), bf16),
        ],
        [pltpu.VMEM((2 * rows, width), bf16), pltpu.VMEM((rows, LANES), bf16)],
        8 * rows * width * width,
        16 * frames * rows,
    )


def temporal_back_kernel(
    need, done, side, valid, ci0, ci1, own, came, mods, stream2, branch, wo0, wo1, qkv, probs,
    wi0, wi1, stream,
    out_near, out_far, rows, dqkv0, dqkv1, grad_near, delta_far, dmod, grad, stack, small,
):
    width, cols, frames = stream.shape[1], wo0.shape[0], mods.shape[0]
    n = stream.shape[0] // frames
    at = [pl.ds(f * n, n) for f in range(frames)]
    gather, spread = head_maps(width)

    def cotangent(f):
        source = ci0 if f < frames // 2 else ci1
        start = (2 * (f % (frames // 2)) + side[0]) * n
        return source[pl.ds(pl.multiple_of(start, n), n), :].astype(f32)

    def put(f, i, value):
        dmod[f : f + 1, i * width : (i + 1) * width] = value

    need(0, 1, 2, 3, 4, 5, 6)
    for f in range(frames):
        m = Mods(mods, valid, f, 2, width)
        s, g = stream2[at[f], :], cotangent(f)
        b = own[0, at[f], :] + came[0, at[f], :].astype(f32)
        d = own[1, at[f], :] + came[1, at[f], :].astype(f32)
        normed, inv_std = norm(s)
        out = out_near if f < frames // 2 else out_far
        out[at[f % (frames // 2)], :] = (s + m.gate * b).astype(bf16)
        put(f, 3, column_sum(d))
        put(f, 4, column_sum(d * normed))
        put(f, 5, column_sum(b * g) * m.valid)
        g = g + norm_back(d, normed, inv_std, m.scale1)
        grad[at[f], :] = g
        m = Mods(mods, valid, f, 1, width)
        put(f, 2, column_sum(g * branch[at[f], :].astype(f32)) * m.valid)
        rows[at[f], :] = (g * m.gate).astype(bf16)
    done(0, 1, 2)
    need(7, 8, 9, 10)
    context_grad = [dot(rows[...], w[...], NT) for w in (wo0, wo1)]

    def store(f, i, value):
        value = value.astype(bf16)
        dqkv0[at[f], i * cols : (i + 1) * cols] = value[:, :cols]
        dqkv1[at[f], i * cols : (i + 1) * cols] = value[:, cols:]

    dk, dv = [0.0] * frames, [0.0] * frames
    for f in range(frames):
        d = jnp.concatenate([c[f * n : (f + 1) * n] for c in context_grad], axis=1)
        d = d.astype(bf16).astype(f32)
        prob_grad = head_sums(
            [d * qkv[2, at[g], :].astype(f32) for g in range(frames)], gather, stack
        )
        p = [probs[f * frames + g] for g in range(frames)]
        p32 = [a.astype(f32) for a in p]
        total = sum(a * b for a, b in zip(prob_grad, p32))
        for g in range(frames):
            small[g * n : (g + 1) * n, :] = (p32[g] * (prob_grad[g] - total)).astype(bf16)
            small[(frames + g) * n : (frames + g + 1) * n, :] = p[g]
        spread_all = dot(small[...], spread)
        q = qkv[0, at[f], :].astype(f32)
        dq = 0.0
        for g in range(frames):
            ds = spread_all[g * n : (g + 1) * n]
            dq = dq + ds * qkv[1, at[g], :].astype(f32)
            dk[g] = dk[g] + ds * q
            dv[g] = dv[g] + spread_all[(frames + g) * n : (frames + g + 1) * n] * d
        store(f, 0, dq * SCALE)
    for g in range(frames):
        store(g, 1, dk[g])
        store(g, 2, dv[g])
    done(3, 4)
    need(11, 12, 13)
    inputs = input_sum((dqkv0, dqkv1), (wi0, wi1))
    for f in range(frames):
        m = Mods(mods, valid, f, 1, width)
        d = inputs[f * n : (f + 1) * n]
        normed, inv_std = norm(stream[at[f], :])
        put(f, 0, column_sum(d))
        put(f, 1, column_sum(d * normed))
        new = grad[at[f], :] + norm_back(d, normed, inv_std, m.scale1)
        if f < frames // 2:
            grad_near[at[f], :] = new
        else:
            delta_far[at[f - frames // 2], :] = (new - cotangent(f)).astype(bf16)
    done(5, 6, 7)


def temporal_back(
    side, valid, ci0, ci1, own, came, mods, stream, stream2, qkv, probs, branch, wi, wo
):
    rows, width = stream.shape
    frames, cols = mods.shape[0], wo[0].shape[0]
    return staged(
        temporal_back_kernel,
        [side, valid],
        [Far(ci0), Far(ci1), own, came, mods]
        + [Far(a) for a in (stream2, branch, *wo, qkv, probs, *wi, stream)],
        [
            Far(shape((rows // 2, width), bf16)),
            Far(shape((rows // 2, width), bf16)),
            shape((rows, width), bf16),
            shape((rows, 3 * cols), bf16),
            shape((rows, 3 * cols), bf16),
            shape((rows // 2, width), f32),
            shape((rows // 2, width), bf16),
            shape((frames, 6 * width), f32),
        ],
        [
            pltpu.VMEM((rows, width), f32),
            pltpu.VMEM((2 * rows, width), bf16),
            pltpu.VMEM((2 * rows, LANES), bf16),
        ],
        8 * rows * width * width,
    )


def gelu_both(u):
    k = 0.7978845608028654
    squared = u * u
    th = jnp.tanh(u * (k + (k * 0.044715) * squared))
    half = 0.5 * (1.0 + th)
    return u * half, half + (0.5 * u) * (1.0 - th * th) * (k + (3 * k * 0.044715) * squared)


def feed_kernel(
    need, done, side, valid, order, s0, s1, ci0, ci1, mods, wu, wd,
    keep, send, acc0, away, r0, r1, acc1, inner, outer,
):
    width, hidden, frames = s0.shape[1], wu.shape[1], mods.shape[0]
    n, chunk, size = s0.shape[0] // frames, inner.shape[1], width // BLOCKS
    acc0[...] = jnp.zeros_like(acc0)
    acc1[...] = jnp.zeros_like(acc1)
    need(0, 1, 2, 3, 4)
    for f in range(frames):
        m = Mods(mods, valid, f, 2, width)
        g = f % (frames // 2)
        source = ci0 if f < frames // 2 else ci1
        here = pl.ds(pl.multiple_of((2 * g + side[0]) * n, n), n)
        there = pl.ds(pl.multiple_of((2 * g + 1 - side[0]) * n, n), n)
        r0[f * n : (f + 1) * n, :] = (m.gate * source[here, :].astype(f32)).astype(bf16)
        to = (f + frames // 2) % frames
        r1[to * n : (to + 1) * n, :] = (m.gate * source[there, :].astype(f32)).astype(bf16)
    need(5, 6)

    def step(i):
        at = slice(i * chunk, (i + 1) * chunk)
        up, down = wu[:, at], wd[at, :]
        up_grad = down_grad = 0.0
        for s, r, acc in ((s0, r0, acc0), (s1, r1, acc1)):
            act, slope = gelu_both(dot(s[...], up))
            act = act.astype(bf16)
            pre_grad = (slope * dot(r[...], down, NT)).astype(bf16)
            acc[0] += dot(act, down)
            acc[1] += dot(pre_grad, up, NT)
            up_grad = up_grad + dot(s[...], pre_grad, TN)
            down_grad = down_grad + dot(r[...], act, TN)
        inner[...] = up_grad.astype(bf16)
        outer[...] = down_grad.astype(bf16)
        for p in range(BLOCKS):
            out, to = (keep, p) if p < BLOCKS // 2 else (send, p - BLOCKS // 2)
            rows = pl.ds(pl.multiple_of(order[p] * size, size), size)
            out[2 * to * size : (2 * to + 1) * size, at] = inner[rows, :]
            out[(2 * to + 1) * size : (2 * to + 2) * size, at] = outer[rows, :]

    for i in range(hidden // chunk):
        step(i)
        done(0, 1, at=(slice(None), pl.ds(i * chunk, chunk)))
    away[...] = acc1[...].astype(bf16)


def feed(side, valid, order, sub, cots, mods, wu, wd):
    rows, width = sub[0].shape
    hidden, chunk = wu.shape[1], 256
    return staged(
        feed_kernel,
        [side, valid, order],
        [*sub, *(Far(c) for c in cots), mods, Far(wu), Far(wd)],
        [
            Far(shape((width, hidden), bf16)),
            Far(shape((width, hidden), bf16)),
            shape((2, rows, width), f32),
            shape((2, rows, width), bf16),
        ],
        [
            pltpu.VMEM((rows, width), bf16),
            pltpu.VMEM((rows, width), bf16),
            pltpu.VMEM((2, rows, width), f32),
            pltpu.VMEM((width, chunk), bf16),
            pltpu.VMEM((width, chunk), bf16),
        ],
        24 * rows * width * hidden,
        2 * rows * hidden,
    )


def condition_kernel(first_block, x, w, out, parts, blocks, sems):
    n, width = x.shape[0], out.shape[0]
    count = x.shape[1] // width
    copies = [
        pltpu.make_async_copy(
            w.at[:, pl.ds((first_block + i) * width, width)], blocks.at[i], sems.at[i]
        )
        for i in range(count)
    ]
    for c in copies:
        c.start()
    total = 0.0
    for i in range(count):
        y = x[:, i * width : (i + 1) * width]
        hi = y.astype(bf16).astype(f32)
        mid = (y - hi).astype(bf16).astype(f32)
        for j, part in enumerate((hi, mid, y - hi - mid, jnp.zeros_like(y))):
            parts[j * n : (j + 1) * n, :] = part
        copies[i].wait()
        total = total + dot(blocks[i], parts[...].astype(bf16), NT)
    out[...] = total


def condition_rows(x, w, first_block):
    n, width = x.shape[0], w.shape[0]
    count = x.shape[1] // width
    out = call(
        functools.partial(condition_kernel, first_block),
        8 * n * width * x.shape[1],
        2 * width * x.shape[1],
        ROOM + 2 * width * x.shape[1],
        in_specs=[VM, pl.BlockSpec(memory_space=pltpu.HBM)],
        out_specs=VM,
        out_shape=shape((width, 4 * n), f32),
        scratch_shapes=[
            pltpu.VMEM((4 * n, width), f32),
            pltpu.VMEM((count, width, width), bf16),
            pltpu.SemaphoreType.DMA((count,)),
        ],
    )(x, in_hbm(w))
    return out.reshape(width, 4, n).sum(axis=1)


def local(
    patches_in, cotangent, condition, frame_clip, frame_valid, w_ada, sp_qkv, sp_out, tm_qkv, tm_out, w_up, w_down,
    dp_size,
):
    frames, patches, width = patches_in.shape
    clips = condition.shape[0]
    t = lax.axis_index("tensor")
    d = lax.axis_index("dp")
    first = t == 0

    def swap(a):
        return lax.ppermute(a, "tensor", [(0, 1), (1, 0)])

    def own_first(a):
        return jnp.where(first, a, jnp.concatenate([a[frames:], a[:frames]], axis=0))

    fence = lax.optimization_barrier
    sq, so, tq, to = ((w, swap(w)) for w in (sp_qkv, sp_out, tm_qkv, tm_out))
    x, cot = patches_in.reshape(-1, width), cotangent.reshape(-1, width)
    x_other, cot_other = swap(x), swap(cot)
    clip_ids = own_first(frame_clip)
    valid_ids = own_first(frame_valid)
    onehot = (clip_ids[:, None] == jnp.arange(clips, dtype=jnp.int32)[None, :]).astype(f32)
    cond_rows = jnp.dot(onehot, condition, precision=highest)
    act_low = jax.nn.silu(cond_rows).astype(bf16)
    mods = jnp.dot(act_low, w_ada, preferred_element_type=f32)
    side, valid = t.reshape(1), valid_ids.astype(f32)
    allowed = (clip_ids[:, None] == clip_ids[None, :]) & (valid_ids[None, :] == 1) | jnp.eye(
        2 * frames, dtype=bool
    )
    bias = jnp.where(allowed, 0.0, -1e30)

    bit0, bit1, rest, outer = d % 2, d // 2 % 2, d // 4, dp_size // 4
    halving = dp_size == BLOCKS
    p = jnp.arange(BLOCKS, dtype=jnp.int32)
    order = p
    if halving:
        hi, mid = p // 8, p // 4 % 2
        far0, far1 = jnp.where(first, hi, mid), jnp.where(first, mid, hi)
        far_z = p // 2 % 2 + 2 * (p % 2)
        order = 4 * (rest ^ far_z) + 2 * (bit1 ^ far1) + (bit0 ^ far0)

    def both_cores(first_bit, second_bit):
        return [(2 * i, 2 * (i ^ first_bit)) for i in range(dp_size)] + [
            (2 * i + 1, 2 * (i ^ second_bit) + 1) for i in range(dp_size)
        ]

    def flip(bits):
        return [(i, i ^ bits) for i in range(dp_size)]

    def across(a, which):
        if not halving:
            return a
        if which < 2:
            pairs = both_cores(*((1, 2) if which == 0 else (2, 1)))
            return lax.ppermute(a, ("dp", "tensor"), pairs)
        return lax.ppermute(a, "dp", flip(4 if which == 2 else 8))

    def fold(keep, came):
        if not halving:
            return keep, came
        n = keep.shape[0] // 2
        return keep[:n] + came[:n], keep[n:] + came[n:]

    def gather_z(keep, came):
        if not halving:
            return [keep, came]
        n = keep.shape[0] // 4
        return [keep[i * n : (i + 1) * n] + came[i * n : (i + 1) * n] for i in range(4)]

    def spread_z(pieces):
        if not halving:
            return pieces
        return pieces[:1] + [
            lax.ppermute(pieces[i], "dp", flip(4 * k)) for i, k in ((2, 1), (1, 2), (3, 3))
        ]

    def finish(pieces):
        if not halving:
            a = jnp.concatenate(pieces, axis=0).astype(f32)
            return lax.psum_scatter(a, "dp", scatter_dimension=0, tiled=True)
        return sum(a.astype(f32) for a in pieces)

    def feed_finish(pieces):
        if halving:
            return finish(pieces).reshape(2, width // dp_size, -1)
        a = jnp.concatenate(pieces, axis=0).astype(f32)
        a = a.reshape(BLOCKS, 2, width // BLOCKS, -1).transpose(1, 0, 2, 3).reshape(2, width, -1)
        return lax.psum_scatter(a, "dp", scatter_dimension=1, tiled=True)

    sub0, qkv0, probs0, *ctx0, branch0, near, far = spatial(
        side, valid, x, mods, sq, so
    )
    stream1, sub1, qkv1, probs1, *ctx1, branch1, stream2, sub2 = temporal(
        side, valid, bias, x, x_other, near, swap(far), mods, tq, to
    )
    mk, ms, sum0, away = feed(
        side, valid, order, (sub2, swap(sub2)), (cot, cot_other), mods, w_up, w_down
    )
    mr = across(ms, 0)
    out_near, out_far, rows1, *dqkv1, grad_near, delta, dmod12 = temporal_back(
        side, valid, cot, cot_other, sum0, swap(away), mods, stream1, stream2, qkv1, probs1,
        branch1, tq, to,
    )
    grad, rows0, *dqkv0, dgate0 = spatial_back(
        side, valid, grad_near, swap(delta), cot, mods, qkv0, probs0, ctx0, branch0, so
    )
    mr, dqkv0 = fence((mr, dqkv0))
    mk, ms = fold(mk, mr)
    mk, ms, dqkv1, dqkv0 = fence((mk, ms, dqkv1, dqkv0))
    mr = across(ms, 1)
    tk, ts = weights(
        order, (sub1, swap(sub1)), (dqkv1[0], swap(dqkv1[1])), (rows1, swap(rows1)),
        (ctx1[0], swap(ctx1[1])),
    )
    tk, ts, dqkv0 = fence((tk, ts, dqkv0))
    tr = across(ts, 0)
    sk, ss = weights(
        order, (sub0, swap(sub0)), (dqkv0[0], swap(dqkv0[1])), (rows0, swap(rows0)),
        (ctx0[0], swap(ctx0[1])),
    )
    sr = across(ss, 0)
    mr, sk = fence((mr, sk))
    mk, ms = fold(mk, mr)
    mk, ms, grad = fence((mk, ms, grad))
    mr = across(ms, 2)
    grad, patches_out, dmod0 = spatial_input(
        side, valid, grad, mods, x, out_near, swap(out_far), dqkv0, sq
    )
    tr, dmod0 = fence((tr, dmod0))
    tk, ts = fold(tk, tr)
    tk, ts, dmod0 = fence((tk, ts, dmod0))
    tr = across(ts, 1)
    late = jnp.concatenate([dmod0, dgate0], axis=1)
    mine = jnp.concatenate([late, dmod12[:frames] + swap(dmod12[frames:])], axis=1)
    act_grad = condition_rows(mine, w_ada, 0).T
    unused, silu_back = jax.vjp(jax.nn.silu, cond_rows[:frames])
    cond_term = silu_back(act_grad)[0]
    sr, cond_term = fence((sr, cond_term))
    sk, ss = fold(sk, sr)
    mr, ss = fence((mr, ss))
    sr = across(ss, 1)
    mk, ms = fold(mk, mr)
    tr, ms = fence((tr, ms))
    mr = across(ms, 3)
    tk, ts = fold(tk, tr)
    sr, ts = fence((sr, ts))
    tr = across(ts, 2)
    pieces = gather_z(sk, sr)
    pieces, cond_term, mine = fence((pieces, cond_term, mine))
    s4 = spread_z(pieces)
    devices = 2 * dp_size
    own_ids = clip_ids[:frames].astype(f32)
    payload = jnp.concatenate(
        [
            mine.reshape(frames, devices, -1),
            cond_term.reshape(frames, devices, -1),
            jnp.broadcast_to(own_ids[:, None, None], (frames, devices, 1)),
        ],
        axis=2,
    )
    got = lax.all_to_all(
        payload.transpose(1, 0, 2), ("dp", "tensor"), split_axis=0, concat_axis=0, tiled=True
    ).reshape(devices * frames, -1)
    tk, ts = fold(tk, tr)
    tr = across(ts, 3)
    ada_cols = 9 * width // devices
    ids = got[:, -1].astype(jnp.int32)
    every = (ids[:, None] == jnp.arange(clips, dtype=jnp.int32)[None, :]).astype(f32)
    act_all = jnp.dot(
        every, jax.nn.silu(condition).astype(bf16).astype(f32), precision=highest
    )
    ada_grad = jnp.dot(act_all.T, got[:, :ada_cols], precision=highest)
    condition_grad = jnp.dot(every.T, got[:, ada_cols:-1], precision=highest)

    def attention_grads(a):
        a = a.reshape(a.shape[0], 4, -1).transpose(1, 0, 2)
        return a[:3], a[3].T

    up_out, down_out = feed_finish([mk, mr])
    return (
        patches_out.reshape(patches_in.shape),
        grad.reshape(patches_in.shape),
        condition_grad,
        ada_grad,
        *attention_grads(finish(s4)),
        *attention_grads(finish([tk, tr])),
        up_out,
        down_out.T,
    )


def solution(mesh):
    return jax.shard_map(
        functools.partial(local, dp_size=mesh.shape["dp"]),
        mesh=mesh,
        in_specs=(
            P(("dp", "tensor"), None, None),
            P(("dp", "tensor"), None, None),
            P(),
            P("dp"),
            P("dp"),
            P(),
            P(None, None, "tensor"),
            P("tensor", None),
            P(None, None, "tensor"),
            P("tensor", None),
            P(None, "tensor"),
            P("tensor", None),
        ),
        out_specs=(
            P(("dp", "tensor"), None, None),
            P(("dp", "tensor"), None, None),
            P(None, ("dp", "tensor")),
            P(None, ("dp", "tensor")),
            P(None, "dp", "tensor"),
            P("tensor", "dp"),
            P(None, "dp", "tensor"),
            P("tensor", "dp"),
            P("dp", "tensor"),
            P("tensor", "dp"),
        ),
        check_vma=False,
    )
```

```python
import functools
import math

import jax
import jax.numpy as jnp
from jax import lax
from jax.experimental import pallas as pl
from jax.experimental.pallas import tpu as pltpu
from jax.sharding import PartitionSpec as P

HD = 64
LANES = 128
SCALE = HD**-0.5
f32 = jnp.float32
bf16 = jnp.bfloat16
highest = lax.Precision.HIGHEST
epsilon = 1e-06
ROOM = 12 * 2**20
PIECES = 6
NN = (((1,), (0,)), ((), ()))
NT = (((1,), (1,)), ((), ()))
TN = (((0,), (0,)), ((), ()))
VM = pl.BlockSpec(memory_space=pltpu.VMEM)
SM = pl.BlockSpec(memory_space=pltpu.SMEM)
shape = jax.ShapeDtypeStruct


def dot(a, b, dims=NN):
    return lax.dot_general(a, b, dims, preferred_element_type=f32)


def norm(x):
    centred = x - jnp.mean(x, -1, keepdims=True)
    inv_std = lax.rsqrt(jnp.mean(centred * centred, -1, keepdims=True) + epsilon)
    return centred * inv_std, inv_std


def norm_back(input_grad, normed, inv_std, scale1):
    d = input_grad * scale1
    return inv_std * (
        d - jnp.mean(d, -1, keepdims=True) - normed * jnp.mean(d * normed, -1, keepdims=True)
    )


def column_sum(x):
    return jnp.sum(x, 0, keepdims=True)


def whole(dims):
    return pl.BlockSpec(dims, lambda *at: (0,) * len(dims))


def call(kernel, flops, bytes_accessed, limit, exps=0, **options):
    return pl.pallas_call(
        kernel,
        compiler_params=pltpu.CompilerParams(vmem_limit_bytes=limit),
        cost_estimate=pl.CostEstimate(
            flops=flops // 100, bytes_accessed=bytes_accessed // 100, transcendentals=exps // 100
        ),
        **options,
    )


def in_hbm(a):
    return pltpu.with_memory_space_constraint(a, pltpu.HBM)


def size_of(a):
    return math.prod(a.shape) * jnp.dtype(a.dtype).itemsize


class Far:
    def __init__(self, array):
        self.array = array


def staged(body, small, ins, outs, scratch, flops, exps=0):
    ns, ni, no = len(small), len(ins), len(outs)
    far_i = [i for i in range(ni) if isinstance(ins[i], Far)]
    far_o = [i for i in range(no) if isinstance(outs[i], Far)]
    ins = [a.array if isinstance(a, Far) else a for a in ins]
    outs = [a.array if isinstance(a, Far) else a for a in outs]

    def kernel(*refs):
        few, refs = refs[:ns], refs[ns:]
        in_refs, out_refs, refs = list(refs[:ni]), list(refs[ni : ni + no]), refs[ni + no :]
        near_i, near_o = refs[: len(far_i)], refs[len(far_i) : len(far_i) + len(far_o)]
        rest, in_sems, out_sems = refs[len(far_i) + len(far_o) : -2], refs[-2], refs[-1]
        copies, results, started = {}, {}, []
        for k, i in enumerate(far_i):
            copies[i] = pltpu.make_async_copy(in_refs[i], near_i[k], in_sems.at[k])
            copies[i].start()
            in_refs[i] = near_i[k]
        for k, i in enumerate(far_o):
            results[i] = (near_o[k], out_refs[i])
            out_refs[i] = near_o[k]

        def need(*which):
            for i in which:
                if i in copies:
                    copies[i].wait()

        def done(*which, at=slice(None)):
            for i in which:
                if i in results:
                    source, target = (r.at[at] for r in results[i])
                    copy = pltpu.make_async_copy(source, target, out_sems.at[len(started)])
                    copy.start()
                    started.append(copy)

        body(need, done, *few, *in_refs, *out_refs, *rest)
        for c in started:
            c.wait()

    far = pl.BlockSpec(memory_space=pltpu.HBM)
    kept = [pltpu.VMEM(ins[i].shape, ins[i].dtype) for i in far_i]
    kept += [pltpu.VMEM(outs[i].shape, outs[i].dtype) for i in far_o]
    own = [a for a in scratch if hasattr(a, "shape")]
    return call(
        kernel,
        flops,
        sum(size_of(a) for a in (*ins, *outs)),
        ROOM + sum(size_of(a) for a in (*kept, *own)),
        exps,
        in_specs=[SM] * ns + [far if i in far_i else VM for i in range(ni)],
        out_specs=[far if i in far_o else VM for i in range(no)],
        out_shape=[
            pltpu.HBM(a.shape, a.dtype) if i in far_o else a for i, a in enumerate(outs)
        ],
        scratch_shapes=kept
        + scratch
        + [
            pltpu.SemaphoreType.DMA((max(1, len(far_i)),)),
            pltpu.SemaphoreType.DMA((PIECES * max(1, len(far_o)),)),
        ],
    )(*small, *(in_hbm(a) if i in far_i else a for i, a in enumerate(ins)))


def head_masks():
    lane = lax.broadcasted_iota(jnp.int32, (1, LANES), 1)
    return [(lane < HD).astype(bf16), (lane >= HD).astype(bf16)]


class Mods:
    def __init__(self, mods, valid, f, b, width):
        def row(i):
            return mods[pl.ds(f, 1), (3 * b + i) * width : (3 * b + i + 1) * width]

        self.shift, self.scale1 = row(0), 1.0 + row(1)
        self.valid = valid[f]
        self.gate = row(2) * self.valid


def project(sub, weights, qkv, rows=slice(None)):
    cols = weights[0].shape[2]
    for h, w in enumerate(weights):
        for i in range(3):
            y = dot(sub, w[i])
            if i == 0:
                y = y * SCALE
            qkv[i, rows, h * cols : (h + 1) * cols] = y.astype(bf16)


def input_sum(dqkv, weights, rows=slice(None)):
    cols, g = weights[0].shape[2], 0.0
    for d, w in zip(dqkv, weights):
        for i in range(3):
            g = g + dot(d[rows, i * cols : (i + 1) * cols], w[i], NT)
    return g


def spatial_kernel(
    need, done, side, valid, x, mods, wi0, wi1, wo0, wo1, sub, qkv, probs, ctx0, ctx1, branch, near, far
):
    frames = valid.shape[0] // 2
    n, width = x.shape[0] // frames, x.shape[1]
    cols, half = wi0.shape[2], n // 2
    masks = head_masks()
    need(0, 1)
    for f in range(frames):
        here = slice(f * n, (f + 1) * n)
        m = Mods(mods, valid, f, 0, width)
        normed, _ = norm(x[here, :].astype(f32))
        sub[here, :] = (normed * m.scale1 + m.shift).astype(bf16)
    done(0)
    for f in range(frames):
        here = slice(f * n, (f + 1) * n)
        if f == 0:
            need(2, 3)
        project(sub[here, :], (wi0, wi1), qkv, here)
        for h, ctx in enumerate((ctx0, ctx1)):
            for j in range(cols // LANES):
                low = slice(j * LANES, (j + 1) * LANES)
                at = slice(h * cols + j * LANES, h * cols + (j + 1) * LANES)
                q, k, v = qkv[0, here, at], qkv[1, here, at], qkv[2, here, at]
                out = 0.0
                for a in range(2):
                    scores = dot(q * masks[a], k, NT)
                    e = jnp.exp(scores - jnp.max(scores, -1, keepdims=True))
                    p = (e * (1.0 / jnp.sum(e, -1, keepdims=True))).astype(bf16)
                    probs[f * (width // HD) + h * (cols // HD) + 2 * j + a] = p
                    out = out + dot(p, v * masks[a])
                ctx[here, low] = out.astype(bf16)
        heads = width // HD
        done(2, at=pl.ds(f * heads, heads))
        done(3, 4, at=pl.ds(f * n, n))
        if f == frames - 1:
            done(1)
        if f == 0:
            need(4, 5)
        y = dot(ctx0[here, :], wo0[...]) + dot(ctx1[here, :], wo1[...])
        branch[here, :] = y.astype(bf16)
        to = slice(f * half, (f + 1) * half)
        near[to, :] = branch[pl.ds(pl.multiple_of(f * n + side[0] * half, half), half), :]
        far[to, :] = branch[pl.ds(pl.multiple_of(f * n + (1 - side[0]) * half, half), half), :]
    done(5)


def spatial(side, valid, x, mods, wi, wo):
    rows, width = x.shape
    frames, heads, cols = valid.shape[0] // 2, width // HD, wo[0].shape[0]
    n = rows // frames
    return staged(
        spatial_kernel,
        [side, valid],
        [Far(x), mods, *(Far(w) for w in (*wi, *wo))],
        [
            Far(shape((rows, width), bf16)),
            Far(shape((3, rows, width), bf16)),
            Far(shape((frames * heads, n, n), bf16)),
            Far(shape((rows, cols), bf16)),
            Far(shape((rows, cols), bf16)),
            Far(shape((rows, width), bf16)),
            shape((rows // 2, width), bf16),
            shape((rows // 2, width), bf16),
        ],
        [],
        rows * width * (8 * width + 4 * n),
        frames * heads * n * n,
    )


def spatial_back_kernel(
    need, done, side, valid, near, far, cot, mods, qkv, probs, ctx0, ctx1, branch, wo0, wo1,
    grad, rows, dqkv0, dqkv1, dgate,
):
    frames = valid.shape[0] // 2
    n, width = cot.shape[0] // frames, cot.shape[1]
    cols, half = wo0.shape[0], n // 2
    masks = head_masks()
    need(0, 1, 2, 3, 8, 9, 10)
    for f in range(frames):
        all_rows = slice(f * n, (f + 1) * n)
        m = Mods(mods, valid, f, 0, width)
        source = slice(f * half, (f + 1) * half)
        here = pl.ds(pl.multiple_of(f * n + side[0] * half, half), half)
        there = pl.ds(pl.multiple_of(f * n + (1 - side[0]) * half, half), half)
        grad[here, :] = near[source, :]
        grad[there, :] = cot[there, :].astype(f32) + far[source, :].astype(f32)
        g = grad[all_rows, :]
        dgate[f : f + 1, :] = column_sum(g * branch[all_rows, :].astype(f32)) * m.valid
        rows[all_rows, :] = (g * m.gate).astype(bf16)
    context_grads = [dot(rows[...], w[...], NT).astype(bf16) for w in (wo0, wo1)]
    need(4, 5, 6, 7)
    for f in range(frames):
        all_rows = slice(f * n, (f + 1) * n)
        for h, (ctx, dqkv) in enumerate(((ctx0, dqkv0), (ctx1, dqkv1))):
            for j in range(cols // LANES):
                low = slice(j * LANES, (j + 1) * LANES)
                at = slice(h * cols + j * LANES, h * cols + (j + 1) * LANES)
                q, k, v = qkv[0, all_rows, at], qkv[1, all_rows, at], qkv[2, all_rows, at]
                d = context_grads[h][all_rows, low]
                product = d.astype(f32) * ctx[all_rows, low].astype(f32)
                dq = dk = dv = 0.0
                for a in range(2):
                    da = d * masks[a]
                    p = probs[f * (width // HD) + h * (cols // HD) + 2 * j + a]
                    delta = jnp.sum(product * masks[a].astype(f32), -1, keepdims=True)
                    ds = (p.astype(f32) * (dot(da, v, NT) - delta)).astype(bf16)
                    dv = dv + dot(p, da, TN)
                    dq = dq + dot(ds, k * masks[a])
                    dk = dk + dot(ds, q * masks[a], TN)
                for i, y in enumerate((dq * SCALE, dk, dv)):
                    to = i * cols + j * LANES
                    dqkv[all_rows, to : to + LANES] = y.astype(bf16)


def spatial_back(side, valid, near, far, cot, mods, qkv, probs, ctx, branch, wo):
    rows, width = cot.shape
    frames, cols = valid.shape[0] // 2, wo[0].shape[0]
    n = rows // frames
    return staged(
        spatial_back_kernel,
        [side, valid],
        [near, far, Far(cot), mods, *(Far(a) for a in (qkv, probs, *ctx, branch, *wo))],
        [
            shape((rows, width), f32),
            shape((rows, width), bf16),
            shape((rows, 3 * cols), bf16),
            shape((rows, 3 * cols), bf16),
            shape((frames, width), f32),
        ],
        [],
        rows * width * (2 * width + 10 * n),
    )


def spatial_input_kernel(
    need, done, side, valid, grad, mods, x, near, far, dqkv0, dqkv1, wi0, wi1, out, layer_out, dmod
):
    frames = valid.shape[0] // 2
    n, width = x.shape[0] // frames, x.shape[1]
    half = n // 2
    need(7, 8)
    inputs = input_sum((dqkv0, dqkv1), (wi0, wi1))
    need(0, 1, 2, 3, 4, 5, 6)
    for f in range(frames):
        m = Mods(mods, valid, f, 0, width)
        here = pl.ds(pl.multiple_of(f * n + side[0] * half, half), half)
        there = pl.ds(pl.multiple_of(f * n + (1 - side[0]) * half, half), half)
        layer_out[here, :] = near[f * half : (f + 1) * half, :]
        layer_out[there, :] = far[f * half : (f + 1) * half, :]
        at = slice(f * n, (f + 1) * n)
        g = inputs[at]
        normed, inv_std = norm(x[at, :].astype(f32))
        dmod[f : f + 1, :width] = column_sum(g)
        dmod[f : f + 1, width:] = column_sum(g * normed)
        out[at, :] = grad[at, :] + norm_back(g, normed, inv_std, m.scale1)
    done(0, 1, 2)


def spatial_input(side, valid, grad, mods, x, near, far, dqkv, wi):
    rows, width = x.shape
    return staged(
        spatial_input_kernel,
        [side, valid],
        [grad, mods, Far(x), Far(near), Far(far), *dqkv, *(Far(w) for w in wi)],
        [
            Far(shape((rows, width), f32)),
            Far(shape((rows, width), bf16)),
            shape((valid.shape[0] // 2, 2 * width), f32),
        ],
        [],
        6 * rows * width * width,
    )


BLOCKS = 16


def store_ordered(order, scratch, keep, send, columns):
    size = scratch.shape[0] // BLOCKS
    for p in range(BLOCKS):
        out = keep if p < BLOCKS // 2 else send
        to = (p % (BLOCKS // 2)) * size
        at = pl.ds(pl.multiple_of(order[p] * size, size), size)
        out[to : to + size, columns] = scratch[at, :]


def weights_kernel(need, done, order, s0, d0, s1, d1, r0, c0, r1, c1, keep, send, wide, narrow):
    split = d0.shape[1]
    need(0, 1)
    total = dot(s0[...], d0[...], TN)
    need(2, 3)
    wide[...] = (total + dot(s1[...], d1[...], TN)).astype(bf16)
    store_ordered(order, wide, keep, send, slice(0, split))
    need(4, 5, 6, 7)
    narrow[...] = (dot(r0[...], c0[...], TN) + dot(r1[...], c1[...], TN)).astype(bf16)
    store_ordered(order, narrow, keep, send, slice(split, keep.shape[1]))
    done(0, 1)


def weights(order, sub, dqkv, rows, ctx):
    n, width = sub[0].shape
    split, cols = dqkv[0].shape[1], ctx[0].shape[1]
    return staged(
        weights_kernel,
        [order],
        [Far(sub[0]), dqkv[0], sub[1], dqkv[1], rows[0], Far(ctx[0]), rows[1], ctx[1]],
        [shape((width // 2, split + cols), bf16)] * 2,
        [pltpu.VMEM((width, split), bf16), pltpu.VMEM((width, cols), bf16)],
        4 * n * width * (split + cols),
    )


def head_sums(products, gather, stack):
    n, count = products[0].shape[0], len(products)
    for i, x in enumerate(products):
        hi = x.astype(bf16)
        stack[i * n : (i + 1) * n, :] = hi
        stack[(count + i) * n : (count + i + 1) * n, :] = (x - hi.astype(f32)).astype(bf16)
    y = dot(stack[...], gather)
    return [y[i * n : (i + 1) * n] + y[(count + i) * n : (count + i + 1) * n] for i in range(count)]


def head_maps(width):
    feature = lax.broadcasted_iota(jnp.int32, (width, LANES), 0) // HD
    head = lax.broadcasted_iota(jnp.int32, (width, LANES), 1)
    gather = (feature == head).astype(bf16)
    feature = lax.broadcasted_iota(jnp.int32, (LANES, width), 1) // HD
    head = lax.broadcasted_iota(jnp.int32, (LANES, width), 0)
    return gather, (feature == head).astype(bf16)


def temporal_kernel(
    need, done, side, valid, bias, x0, x1, b0, b1, mods, wi0, wi1, wo0, wo1,
    stream, sub, qkv, probs, ctx0, ctx1, branch, stream2, sub2, stack, small,
):
    rows, width = sub.shape
    cols, frames = wi0.shape[2], mods.shape[0]
    n = rows // frames
    at = [pl.ds(f * n, n) for f in range(frames)]
    need(0, 1, 2, 3, 4)
    for f in range(frames):
        xs, bs = (x0, b0) if f < frames // 2 else (x1, b1)
        g = f % (frames // 2)
        source = pl.ds(pl.multiple_of((2 * g + side[0]) * n, n), n)
        before, m = Mods(mods, valid, f, 0, width), Mods(mods, valid, f, 1, width)
        s = xs[source, :].astype(f32) + before.gate * bs[at[g], :].astype(f32)
        stream[at[f], :] = s
        normed, _ = norm(s)
        sub[at[f], :] = (normed * m.scale1 + m.shift).astype(bf16)
    done(0, 1)
    need(5, 6)
    project(sub[...], (wi0, wi1), qkv)
    done(2)
    gather, spread = head_maps(width)
    for f in range(frames):
        q = qkv[0, at[f], :].astype(f32)
        scores = head_sums(
            [q * qkv[1, at[g], :].astype(f32) for g in range(frames)], gather, stack
        )
        scores = [s + bias[f, g] for g, s in enumerate(scores)]
        top = functools.reduce(jnp.maximum, scores)
        e = [jnp.exp(s - top) for s in scores]
        inv = 1.0 / sum(e)
        for g in range(frames):
            p = (e[g] * inv).astype(bf16)
            probs[f * frames + g] = p
            small[at[g], :] = p
        spread_p = dot(small[...], spread)
        context = sum(
            spread_p[g * n : (g + 1) * n] * qkv[2, at[g], :].astype(f32) for g in range(frames)
        )
        ctx0[at[f], :] = context[:, :cols].astype(bf16)
        ctx1[at[f], :] = context[:, cols:].astype(bf16)
    done(3, 4, 5)
    need(7, 8)
    for f in range(frames):
        m, after = Mods(mods, valid, f, 1, width), Mods(mods, valid, f, 2, width)
        b = dot(ctx0[at[f], :], wo0[...]) + dot(ctx1[at[f], :], wo1[...])
        branch[at[f], :] = b.astype(bf16)
        s = stream[at[f], :] + m.gate * b
        stream2[at[f], :] = s
        normed, _ = norm(s)
        sub2[at[f], :] = (normed * after.scale1 + after.shift).astype(bf16)
    done(6, 7, 8)


def temporal(side, valid, bias, x0, x1, b0, b1, mods, wi, wo):
    rows, width = x0.shape
    frames, cols = mods.shape[0], wo[0].shape[0]
    n = rows // frames
    return staged(
        temporal_kernel,
        [side, valid, bias],
        [Far(x0), Far(x1), b0, b1, mods, *(Far(w) for w in (*wi, *wo))],
        [
            Far(shape((rows, width), f32)),
            Far(shape((rows, width), bf16)),
            Far(shape((3, rows, width), bf16)),
            Far(shape((frames * frames, n, LANES), bf16)),
            Far(shape((rows, cols), bf16)),
            Far(shape((rows, cols), bf16)),
            Far(shape((rows, width), bf16)),
            Far(shape((rows, width), f32)),
            shape((rows, width), bf16),
        ],
        [pltpu.VMEM((2 * rows, width), bf16), pltpu.VMEM((rows, LANES), bf16)],
        8 * rows * width * width,
        16 * frames * rows,
    )


def temporal_back_kernel(
    need, done, side, valid, ci0, ci1, own, came, mods, stream2, branch, wo0, wo1, qkv, probs,
    wi0, wi1, stream,
    out_near, out_far, rows, dqkv0, dqkv1, grad_near, delta_far, dmod, grad, stack, small,
):
    width, cols, frames = stream.shape[1], wo0.shape[0], mods.shape[0]
    n = stream.shape[0] // frames
    at = [pl.ds(f * n, n) for f in range(frames)]
    gather, spread = head_maps(width)

    def cotangent(f):
        source = ci0 if f < frames // 2 else ci1
        start = (2 * (f % (frames // 2)) + side[0]) * n
        return source[pl.ds(pl.multiple_of(start, n), n), :].astype(f32)

    def put(f, i, value):
        dmod[f : f + 1, i * width : (i + 1) * width] = value

    need(0, 1, 2, 3, 4, 5, 6)
    for f in range(frames):
        m = Mods(mods, valid, f, 2, width)
        s, g = stream2[at[f], :], cotangent(f)
        b = own[0, at[f], :] + came[0, at[f], :].astype(f32)
        d = own[1, at[f], :] + came[1, at[f], :].astype(f32)
        normed, inv_std = norm(s)
        out = out_near if f < frames // 2 else out_far
        out[at[f % (frames // 2)], :] = (s + m.gate * b).astype(bf16)
        put(f, 3, column_sum(d))
        put(f, 4, column_sum(d * normed))
        put(f, 5, column_sum(b * g) * m.valid)
        g = g + norm_back(d, normed, inv_std, m.scale1)
        grad[at[f], :] = g
        m = Mods(mods, valid, f, 1, width)
        put(f, 2, column_sum(g * branch[at[f], :].astype(f32)) * m.valid)
        rows[at[f], :] = (g * m.gate).astype(bf16)
    done(0, 1, 2)
    need(7, 8, 9, 10)
    context_grad = [dot(rows[...], w[...], NT) for w in (wo0, wo1)]

    def store(f, i, value):
        value = value.astype(bf16)
        dqkv0[at[f], i * cols : (i + 1) * cols] = value[:, :cols]
        dqkv1[at[f], i * cols : (i + 1) * cols] = value[:, cols:]

    dk, dv = [0.0] * frames, [0.0] * frames
    for f in range(frames):
        d = jnp.concatenate([c[f * n : (f + 1) * n] for c in context_grad], axis=1)
        d = d.astype(bf16).astype(f32)
        prob_grad = head_sums(
            [d * qkv[2, at[g], :].astype(f32) for g in range(frames)], gather, stack
        )
        p = [probs[f * frames + g] for g in range(frames)]
        p32 = [a.astype(f32) for a in p]
        total = sum(a * b for a, b in zip(prob_grad, p32))
        for g in range(frames):
            small[g * n : (g + 1) * n, :] = (p32[g] * (prob_grad[g] - total)).astype(bf16)
            small[(frames + g) * n : (frames + g + 1) * n, :] = p[g]
        spread_all = dot(small[...], spread)
        q = qkv[0, at[f], :].astype(f32)
        dq = 0.0
        for g in range(frames):
            ds = spread_all[g * n : (g + 1) * n]
            dq = dq + ds * qkv[1, at[g], :].astype(f32)
            dk[g] = dk[g] + ds * q
            dv[g] = dv[g] + spread_all[(frames + g) * n : (frames + g + 1) * n] * d
        store(f, 0, dq * SCALE)
    for g in range(frames):
        store(g, 1, dk[g])
        store(g, 2, dv[g])
    done(3, 4)
    need(11, 12, 13)
    inputs = input_sum((dqkv0, dqkv1), (wi0, wi1))
    for f in range(frames):
        m = Mods(mods, valid, f, 1, width)
        d = inputs[f * n : (f + 1) * n]
        normed, inv_std = norm(stream[at[f], :])
        put(f, 0, column_sum(d))
        put(f, 1, column_sum(d * normed))
        new = grad[at[f], :] + norm_back(d, normed, inv_std, m.scale1)
        if f < frames // 2:
            grad_near[at[f], :] = new
        else:
            delta_far[at[f - frames // 2], :] = (new - cotangent(f)).astype(bf16)
    done(5, 6, 7)


def temporal_back(
    side, valid, ci0, ci1, own, came, mods, stream, stream2, qkv, probs, branch, wi, wo
):
    rows, width = stream.shape
    frames, cols = mods.shape[0], wo[0].shape[0]
    return staged(
        temporal_back_kernel,
        [side, valid],
        [Far(ci0), Far(ci1), own, came, mods]
        + [Far(a) for a in (stream2, branch, *wo, qkv, probs, *wi, stream)],
        [
            Far(shape((rows // 2, width), bf16)),
            Far(shape((rows // 2, width), bf16)),
            shape((rows, width), bf16),
            shape((rows, 3 * cols), bf16),
            shape((rows, 3 * cols), bf16),
            shape((rows // 2, width), f32),
            shape((rows // 2, width), bf16),
            shape((frames, 6 * width), f32),
        ],
        [
            pltpu.VMEM((rows, width), f32),
            pltpu.VMEM((2 * rows, width), bf16),
            pltpu.VMEM((2 * rows, LANES), bf16),
        ],
        8 * rows * width * width,
    )


def gelu_both(u):
    k = 0.7978845608028654
    squared = u * u
    th = jnp.tanh(u * (k + (k * 0.044715) * squared))
    half = 0.5 * (1.0 + th)
    return u * half, half + (0.5 * u) * (1.0 - th * th) * (k + (3 * k * 0.044715) * squared)


def feed_kernel(
    need, done, side, valid, order, s0, s1, ci0, ci1, mods, wu, wd,
    keep_a, send_a, keep_b, send_b, acc0, away, r0, r1, acc1, inner, outer,
):
    width, hidden, frames = s0.shape[1], wu.shape[1], mods.shape[0]
    n, chunk, size = s0.shape[0] // frames, inner.shape[1], width // BLOCKS
    acc0[...] = jnp.zeros_like(acc0)
    acc1[...] = jnp.zeros_like(acc1)
    need(0, 1, 2, 3, 4)
    for f in range(frames):
        m = Mods(mods, valid, f, 2, width)
        g = f % (frames // 2)
        source = ci0 if f < frames // 2 else ci1
        here = pl.ds(pl.multiple_of((2 * g + side[0]) * n, n), n)
        there = pl.ds(pl.multiple_of((2 * g + 1 - side[0]) * n, n), n)
        r0[f * n : (f + 1) * n, :] = (m.gate * source[here, :].astype(f32)).astype(bf16)
        to = (f + frames // 2) % frames
        r1[to * n : (to + 1) * n, :] = (m.gate * source[there, :].astype(f32)).astype(bf16)
    need(5, 6)

    def step(i):
        at = slice(i * chunk, (i + 1) * chunk)
        up, down = wu[:, at], wd[at, :]
        up_grad = down_grad = 0.0
        for s, r, acc in ((s0, r0, acc0), (s1, r1, acc1)):
            act, slope = gelu_both(dot(s[...], up))
            act = act.astype(bf16)
            pre_grad = (slope * dot(r[...], down, NT)).astype(bf16)
            acc[0] += dot(act, down)
            acc[1] += dot(pre_grad, up, NT)
            up_grad = up_grad + dot(s[...], pre_grad, TN)
            down_grad = down_grad + dot(r[...], act, TN)
        inner[...] = up_grad.astype(bf16)
        outer[...] = down_grad.astype(bf16)
        low = i * chunk
        if low < keep_a.shape[1]:
            keep, send, first, results = keep_a, send_a, 0, (0, 1)
        else:
            keep, send, first, results = keep_b, send_b, BLOCKS, (2, 3)
            low = low - keep_a.shape[1]
        to_columns = slice(low, low + chunk)
        for p in range(BLOCKS):
            out, to = (keep, p) if p < BLOCKS // 2 else (send, p - BLOCKS // 2)
            rows = pl.ds(pl.multiple_of(order[first + p] * size, size), size)
            out[2 * to * size : (2 * to + 1) * size, to_columns] = inner[rows, :]
            out[(2 * to + 1) * size : (2 * to + 2) * size, to_columns] = outer[rows, :]
        done(*results, at=(slice(None), pl.ds(low, chunk)))

    for i in range(hidden // chunk):
        step(i)
    away[...] = acc1[...].astype(bf16)


def feed(side, valid, order, sub, cots, mods, wu, wd):
    rows, width = sub[0].shape
    hidden, chunk = wu.shape[1], 512
    part_b = hidden // 3 // chunk * chunk
    part_a = hidden - part_b
    return staged(
        feed_kernel,
        [side, valid, order],
        [*sub, *(Far(c) for c in cots), mods, Far(wu), Far(wd)],
        [
            Far(shape((width, part_a), bf16)),
            Far(shape((width, part_a), bf16)),
            Far(shape((width, part_b), bf16)),
            Far(shape((width, part_b), bf16)),
            shape((2, rows, width), f32),
            shape((2, rows, width), bf16),
        ],
        [
            pltpu.VMEM((rows, width), bf16),
            pltpu.VMEM((rows, width), bf16),
            pltpu.VMEM((2, rows, width), f32),
            pltpu.VMEM((width, chunk), bf16),
            pltpu.VMEM((width, chunk), bf16),
        ],
        24 * rows * width * hidden,
        2 * rows * hidden,
    )


def condition_kernel(first_block, x, w, out, parts, blocks, sems):
    n, width = x.shape[0], out.shape[0]
    count = x.shape[1] // width
    copies = [
        pltpu.make_async_copy(
            w.at[:, pl.ds((first_block + i) * width, width)], blocks.at[i], sems.at[i]
        )
        for i in range(count)
    ]
    for c in copies:
        c.start()
    total = 0.0
    for i in range(count):
        y = x[:, i * width : (i + 1) * width]
        hi = y.astype(bf16).astype(f32)
        mid = (y - hi).astype(bf16).astype(f32)
        for j, part in enumerate((hi, mid, y - hi - mid, jnp.zeros_like(y))):
            parts[j * n : (j + 1) * n, :] = part
        copies[i].wait()
        total = total + dot(blocks[i], parts[...].astype(bf16), NT)
    out[...] = total


def condition_rows(x, w, first_block):
    n, width = x.shape[0], w.shape[0]
    count = x.shape[1] // width
    out = call(
        functools.partial(condition_kernel, first_block),
        8 * n * width * x.shape[1],
        2 * width * x.shape[1],
        ROOM + 2 * width * x.shape[1],
        in_specs=[VM, pl.BlockSpec(memory_space=pltpu.HBM)],
        out_specs=VM,
        out_shape=shape((width, 4 * n), f32),
        scratch_shapes=[
            pltpu.VMEM((4 * n, width), f32),
            pltpu.VMEM((count, width, width), bf16),
            pltpu.SemaphoreType.DMA((count,)),
        ],
    )(x, in_hbm(w))
    return out.reshape(width, 4, n).sum(axis=1)


def local(
    patches_in, cotangent, condition, frame_clip, frame_valid, w_ada, sp_qkv, sp_out, tm_qkv, tm_out, w_up, w_down,
    dp_size,
):
    frames, patches, width = patches_in.shape
    clips = condition.shape[0]
    t = lax.axis_index("tensor")
    d = lax.axis_index("dp")
    first = t == 0

    def swap(a):
        return lax.ppermute(a, "tensor", [(0, 1), (1, 0)])

    def own_first(a):
        return jnp.where(first, a, jnp.concatenate([a[frames:], a[:frames]], axis=0))

    fence = lax.optimization_barrier
    sq, so, tq, to = ((w, swap(w)) for w in (sp_qkv, sp_out, tm_qkv, tm_out))
    x, cot = patches_in.reshape(-1, width), cotangent.reshape(-1, width)
    x_other, cot_other = swap(x), swap(cot)
    clip_ids = own_first(frame_clip)
    valid_ids = own_first(frame_valid)
    onehot = (clip_ids[:, None] == jnp.arange(clips, dtype=jnp.int32)[None, :]).astype(f32)
    cond_rows = jnp.dot(onehot, condition, precision=highest)
    act_low = jax.nn.silu(cond_rows).astype(bf16)
    mods = jnp.dot(act_low, w_ada, preferred_element_type=f32)
    side, valid = t.reshape(1), valid_ids.astype(f32)
    allowed = (clip_ids[:, None] == clip_ids[None, :]) & (valid_ids[None, :] == 1) | jnp.eye(
        2 * frames, dtype=bool
    )
    bias = jnp.where(allowed, 0.0, -1e30)

    bit0, bit1, rest, outer = d % 2, d // 2 % 2, d // 4, dp_size // 4
    halving = dp_size == BLOCKS
    p = jnp.arange(BLOCKS, dtype=jnp.int32)
    order = order_b = p

    def order_of(far0, far1, z0, z1):
        bx, by = jnp.where(first, far0, far1), jnp.where(first, far1, far0)
        return 4 * (rest ^ (z0 + 2 * z1)) + 2 * (bit1 ^ by) + (bit0 ^ bx)

    if halving:
        bits = [p // 8, p // 4 % 2, p // 2 % 2, p % 2]
        order = order_of(*bits)
        order_b = order_of(bits[1], bits[2], bits[0], bits[3])
    feed_order = jnp.concatenate([order, order_b])

    def both_cores(first_bit, second_bit):
        return [(2 * i, 2 * (i ^ first_bit)) for i in range(dp_size)] + [
            (2 * i + 1, 2 * (i ^ second_bit) + 1) for i in range(dp_size)
        ]

    def flip(bits):
        return [(i, i ^ bits) for i in range(dp_size)]

    def across(a, which):
        if not halving:
            return a
        if which < 2:
            pairs = both_cores(*((1, 2) if which == 0 else (2, 1)))
            return lax.ppermute(a, ("dp", "tensor"), pairs)
        return lax.ppermute(a, "dp", flip(4 if which == 2 else 8))

    def fold(keep, came):
        if not halving:
            return keep, came
        n = keep.shape[0] // 2
        return keep[:n] + came[:n], keep[n:] + came[n:]

    def gather_z(keep, came):
        if not halving:
            return [keep, came]
        n = keep.shape[0] // 4
        return [keep[i * n : (i + 1) * n] + came[i * n : (i + 1) * n] for i in range(4)]

    def spread_z(pieces):
        if not halving:
            return pieces
        return pieces[:1] + [
            lax.ppermute(pieces[i], "dp", flip(4 * k)) for i, k in ((2, 1), (1, 2), (3, 3))
        ]

    def finish(pieces):
        if not halving:
            a = jnp.concatenate(pieces, axis=0).astype(f32)
            return lax.psum_scatter(a, "dp", scatter_dimension=0, tiled=True)
        return sum(a.astype(f32) for a in pieces)

    def feed_finish(*parts):
        if halving:
            a = jnp.concatenate([finish(pieces) for pieces in parts], axis=1)
            return a.reshape(2, width // dp_size, -1)
        a = jnp.concatenate([jnp.concatenate(pieces, axis=0) for pieces in parts], axis=1)
        a = a.astype(f32).reshape(BLOCKS, 2, width // BLOCKS, -1)
        a = a.transpose(1, 0, 2, 3).reshape(2, width, -1)
        return lax.psum_scatter(a, "dp", scatter_dimension=1, tiled=True)

    sub0, qkv0, probs0, *ctx0, branch0, near, far = spatial(
        side, valid, x, mods, sq, so
    )
    stream1, sub1, qkv1, probs1, *ctx1, branch1, stream2, sub2 = temporal(
        side, valid, bias, x, x_other, near, swap(far), mods, tq, to
    )
    mk, ms, nk, ns, sum0, away = feed(
        side, valid, feed_order, (sub2, swap(sub2)), (cot, cot_other), mods, w_up, w_down
    )
    early = [swap(a) for a in (sub1, ctx1[1])]
    early, away = fence((early, away))
    mr, nr = across(ms, 0), across(ns, 2)
    out_near, out_far, rows1, *dqkv1, grad_near, delta, dmod12 = temporal_back(
        side, valid, cot, cot_other, sum0, swap(away), mods, stream1, stream2, qkv1, probs1,
        branch1, tq, to,
    )
    came1 = [early[0], swap(dqkv1[1]), swap(rows1), early[1]]
    delta, nr = fence((swap(delta), nr))
    nk, ns = fold(nk, nr)
    ns, delta = fence((ns, delta))
    nr = across(ns, 0)
    grad, rows0, *dqkv0, dgate0 = spatial_back(
        side, valid, grad_near, delta, cot, mods, qkv0, probs0, ctx0, branch0, so
    )
    came0 = [swap(a) for a in (sub0, dqkv0[1], rows0, ctx0[1])]
    came1, mr, nr, dqkv0 = fence((came1, mr, nr, dqkv0))
    mk, ms = fold(mk, mr)
    nk, ns = fold(nk, nr)
    ms, ns, came1 = fence((ms, ns, came1))
    mr, nr = across(ms, 1), across(ns, 1)
    tk, ts = weights(
        order, (sub1, came1[0]), (dqkv1[0], came1[1]), (rows1, came1[2]), (ctx1[0], came1[3])
    )
    tr = across(ts, 0)
    came0, mr, ts = fence((came0, mr, ts))
    mk, ms = fold(mk, mr)
    ms, came0 = fence((ms, came0))
    mr = across(ms, 2)
    sk, ss = weights(
        order, (sub0, came0[0]), (dqkv0[0], came0[1]), (rows0, came0[2]), (ctx0[0], came0[3])
    )
    sr = across(ss, 0)
    mr, nr, ss = fence((mr, nr, ss))
    mk, ms = fold(mk, mr)
    nk, ns = fold(nk, nr)
    ms, ns, ss, grad = fence((ms, ns, ss, grad))
    mr, nr = across(ms, 3), across(ns, 3)
    grad, patches_out, dmod0 = spatial_input(
        side, valid, grad, mods, x, out_near, swap(out_far), dqkv0, sq
    )
    tr, dmod0 = fence((tr, dmod0))
    tk, ts = fold(tk, tr)
    ts, dmod0 = fence((ts, dmod0))
    tr = across(ts, 1)
    late = jnp.concatenate([dmod0, dgate0], axis=1)
    mine = jnp.concatenate([late, dmod12[:frames] + swap(dmod12[frames:])], axis=1)
    act_grad = condition_rows(mine, w_ada, 0).T
    tr, sr, mr, nr, act_grad = fence((tr, sr, mr, nr, act_grad))
    sk, ss = fold(sk, sr)
    ss, act_grad, tr = fence((ss, act_grad, tr))
    tk, ts = fold(tk, tr)
    sr, tr = across(ss, 1), across(ts, 2)
    unused, silu_back = jax.vjp(jax.nn.silu, cond_rows[:frames])
    cond_term = silu_back(act_grad)[0]
    sr, tr = fence((sr, tr))
    pieces = gather_z(sk, sr)
    tk, ts = fold(tk, tr)
    pieces, ts, mk, mr, nk, nr, cond_term, mine = fence(
        (pieces, ts, mk, mr, nk, nr, cond_term, mine)
    )
    s4, tr = spread_z(pieces), across(ts, 3)
    devices = 2 * dp_size
    own_ids = clip_ids[:frames].astype(f32)
    payload = jnp.concatenate(
        [
            mine.reshape(frames, devices, -1),
            cond_term.reshape(frames, devices, -1),
            jnp.broadcast_to(own_ids[:, None, None], (frames, devices, 1)),
        ],
        axis=2,
    )
    got = lax.all_to_all(
        payload.transpose(1, 0, 2), ("dp", "tensor"), split_axis=0, concat_axis=0, tiled=True
    ).reshape(devices * frames, -1)
    ada_cols = 9 * width // devices
    ids = got[:, -1].astype(jnp.int32)
    every = (ids[:, None] == jnp.arange(clips, dtype=jnp.int32)[None, :]).astype(f32)
    act_all = jnp.dot(
        every, jax.nn.silu(condition).astype(bf16).astype(f32), precision=highest
    )
    ada_grad = jnp.dot(act_all.T, got[:, :ada_cols], precision=highest)
    condition_grad = jnp.dot(every.T, got[:, ada_cols:-1], precision=highest)

    def attention_grads(a):
        a = a.reshape(a.shape[0], 4, -1).transpose(1, 0, 2)
        return a[:3], a[3].T

    up_out, down_out = feed_finish([mk, mr], [nk, nr])
    return (
        patches_out.reshape(patches_in.shape),
        grad.reshape(patches_in.shape),
        condition_grad,
        ada_grad,
        *attention_grads(finish(s4)),
        *attention_grads(finish([tk, tr])),
        up_out,
        down_out.T,
    )


def solution(mesh):
    return jax.shard_map(
        functools.partial(local, dp_size=mesh.shape["dp"]),
        mesh=mesh,
        in_specs=(
            P(("dp", "tensor"), None, None),
            P(("dp", "tensor"), None, None),
            P(),
            P("dp"),
            P("dp"),
            P(),
            P(None, None, "tensor"),
            P("tensor", None),
            P(None, None, "tensor"),
            P("tensor", None),
            P(None, "tensor"),
            P("tensor", None),
        ),
        out_specs=(
            P(("dp", "tensor"), None, None),
            P(("dp", "tensor"), None, None),
            P(None, ("dp", "tensor")),
            P(None, ("dp", "tensor")),
            P(None, "dp", "tensor"),
            P("tensor", "dp"),
            P(None, "dp", "tensor"),
            P("tensor", "dp"),
            P("dp", "tensor"),
            P("tensor", "dp"),
        ),
        check_vma=False,
    )
```

```python
import functools
import math

import jax
import jax.numpy as jnp
from jax import lax
from jax.experimental import pallas as pl
from jax.experimental.pallas import tpu as pltpu
from jax.sharding import PartitionSpec as P

HD = 64
LANES = 128
SCALE = HD**-0.5
f32 = jnp.float32
bf16 = jnp.bfloat16
highest = lax.Precision.HIGHEST
epsilon = 1e-06
ROOM = 12 * 2**20
PIECES = 6
NN = (((1,), (0,)), ((), ()))
NT = (((1,), (1,)), ((), ()))
TN = (((0,), (0,)), ((), ()))
VM = pl.BlockSpec(memory_space=pltpu.VMEM)
SM = pl.BlockSpec(memory_space=pltpu.SMEM)
shape = jax.ShapeDtypeStruct


def dot(a, b, dims=NN):
    return lax.dot_general(a, b, dims, preferred_element_type=f32)


def norm(x):
    centred = x - jnp.mean(x, -1, keepdims=True)
    inv_std = lax.rsqrt(jnp.mean(centred * centred, -1, keepdims=True) + epsilon)
    return centred * inv_std, inv_std


def norm_back(input_grad, normed, inv_std, scale1):
    d = input_grad * scale1
    return inv_std * (
        d - jnp.mean(d, -1, keepdims=True) - normed * jnp.mean(d * normed, -1, keepdims=True)
    )


def column_sum(x):
    return jnp.sum(x, 0, keepdims=True)


def whole(dims):
    return pl.BlockSpec(dims, lambda *at: (0,) * len(dims))


def call(kernel, flops, bytes_accessed, limit, exps=0, **options):
    return pl.pallas_call(
        kernel,
        compiler_params=pltpu.CompilerParams(vmem_limit_bytes=limit),
        cost_estimate=pl.CostEstimate(
            flops=flops // 100, bytes_accessed=bytes_accessed // 100, transcendentals=exps // 100
        ),
        **options,
    )


def in_hbm(a):
    return pltpu.with_memory_space_constraint(a, pltpu.HBM)


def size_of(a):
    return math.prod(a.shape) * jnp.dtype(a.dtype).itemsize


class Far:
    def __init__(self, array):
        self.array = array


def staged(body, small, ins, outs, scratch, flops, exps=0):
    ns, ni, no = len(small), len(ins), len(outs)
    far_i = [i for i in range(ni) if isinstance(ins[i], Far)]
    far_o = [i for i in range(no) if isinstance(outs[i], Far)]
    ins = [a.array if isinstance(a, Far) else a for a in ins]
    outs = [a.array if isinstance(a, Far) else a for a in outs]

    def kernel(*refs):
        few, refs = refs[:ns], refs[ns:]
        in_refs, out_refs, refs = list(refs[:ni]), list(refs[ni : ni + no]), refs[ni + no :]
        near_i, near_o = refs[: len(far_i)], refs[len(far_i) : len(far_i) + len(far_o)]
        rest, in_sems, out_sems = refs[len(far_i) + len(far_o) : -2], refs[-2], refs[-1]
        copies, results, started = {}, {}, []
        for k, i in enumerate(far_i):
            copies[i] = pltpu.make_async_copy(in_refs[i], near_i[k], in_sems.at[k])
            copies[i].start()
            in_refs[i] = near_i[k]
        for k, i in enumerate(far_o):
            results[i] = (near_o[k], out_refs[i])
            out_refs[i] = near_o[k]

        def need(*which):
            for i in which:
                if i in copies:
                    copies[i].wait()

        def done(*which, at=slice(None)):
            for i in which:
                if i in results:
                    source, target = (r.at[at] for r in results[i])
                    copy = pltpu.make_async_copy(source, target, out_sems.at[len(started)])
                    copy.start()
                    started.append(copy)

        body(need, done, *few, *in_refs, *out_refs, *rest)
        for c in started:
            c.wait()

    far = pl.BlockSpec(memory_space=pltpu.HBM)
    kept = [pltpu.VMEM(ins[i].shape, ins[i].dtype) for i in far_i]
    kept += [pltpu.VMEM(outs[i].shape, outs[i].dtype) for i in far_o]
    own = [a for a in scratch if hasattr(a, "shape")]
    return call(
        kernel,
        flops,
        sum(size_of(a) for a in (*ins, *outs)),
        ROOM + sum(size_of(a) for a in (*kept, *own)),
        exps,
        in_specs=[SM] * ns + [far if i in far_i else VM for i in range(ni)],
        out_specs=[far if i in far_o else VM for i in range(no)],
        out_shape=[
            pltpu.HBM(a.shape, a.dtype) if i in far_o else a for i, a in enumerate(outs)
        ],
        scratch_shapes=kept
        + scratch
        + [
            pltpu.SemaphoreType.DMA((max(1, len(far_i)),)),
            pltpu.SemaphoreType.DMA((PIECES * max(1, len(far_o)),)),
        ],
    )(*small, *(in_hbm(a) if i in far_i else a for i, a in enumerate(ins)))


def pair_rows(x):
    first = lax.broadcasted_iota(jnp.int32, (1, LANES), 1) < HD
    first = first.astype(x.dtype)
    return jnp.concatenate([x * first, x * (1 - first)], axis=0)


def pair_lanes(x):
    n = x.shape[0] // 2
    first = lax.broadcasted_iota(jnp.int32, (1, LANES), 1) < HD
    return jnp.where(first, x[:n], x[n:])


class Mods:
    def __init__(self, mods, valid, f, b, width):
        def row(i):
            return mods[pl.ds(f, 1), (3 * b + i) * width : (3 * b + i + 1) * width]

        self.shift, self.scale1 = row(0), 1.0 + row(1)
        self.valid = valid[f]
        self.gate = row(2) * self.valid


def project(sub, weights, qkv, rows=slice(None)):
    cols = weights[0].shape[2]
    for h, w in enumerate(weights):
        for i in range(3):
            y = dot(sub, w[i])
            if i == 0:
                y = y * SCALE
            qkv[i, rows, h * cols : (h + 1) * cols] = y.astype(bf16)


def input_sum(dqkv, weights, rows=slice(None)):
    cols, g = weights[0].shape[2], 0.0
    for d, w in zip(dqkv, weights):
        for i in range(3):
            g = g + dot(d[rows, i * cols : (i + 1) * cols], w[i], NT)
    return g


def spatial_kernel(
    need, done, side, valid, x, mods, wi0, wi1, wo0, wo1, sub, qkv, probs, ctx0, ctx1, branch, near, far
):
    frames = valid.shape[0] // 2
    n, width = x.shape[0] // frames, x.shape[1]
    cols, half = wi0.shape[2], n // 2
    need(0, 1)
    for f in range(frames):
        here = slice(f * n, (f + 1) * n)
        m = Mods(mods, valid, f, 0, width)
        normed, _ = norm(x[here, :].astype(f32))
        sub[here, :] = (normed * m.scale1 + m.shift).astype(bf16)
    done(0)
    for f in range(frames):
        here = slice(f * n, (f + 1) * n)
        if f == 0:
            need(2, 3)
        project(sub[here, :], (wi0, wi1), qkv, here)
        for h, ctx in enumerate((ctx0, ctx1)):
            for j in range(cols // LANES):
                low = slice(j * LANES, (j + 1) * LANES)
                at = slice(h * cols + j * LANES, h * cols + (j + 1) * LANES)
                q, k, v = qkv[0, here, at], qkv[1, here, at], qkv[2, here, at]
                scores = dot(pair_rows(q), k, NT)
                e = jnp.exp(scores - jnp.max(scores, -1, keepdims=True))
                p = (e * (1.0 / jnp.sum(e, -1, keepdims=True))).astype(bf16)
                head = f * (width // HD) + h * (cols // HD) + 2 * j
                probs[head], probs[head + 1] = p[:n], p[n:]
                ctx[here, low] = pair_lanes(dot(p, v)).astype(bf16)
        heads = width // HD
        done(2, at=pl.ds(f * heads, heads))
        done(3, 4, at=pl.ds(f * n, n))
        if f == frames - 1:
            done(1)
        if f == 0:
            need(4, 5)
        y = dot(ctx0[here, :], wo0[...]) + dot(ctx1[here, :], wo1[...])
        branch[here, :] = y.astype(bf16)
        to = slice(f * half, (f + 1) * half)
        near[to, :] = branch[pl.ds(pl.multiple_of(f * n + side[0] * half, half), half), :]
        far[to, :] = branch[pl.ds(pl.multiple_of(f * n + (1 - side[0]) * half, half), half), :]
    done(5)


def spatial(side, valid, x, mods, wi, wo):
    rows, width = x.shape
    frames, heads, cols = valid.shape[0] // 2, width // HD, wo[0].shape[0]
    n = rows // frames
    return staged(
        spatial_kernel,
        [side, valid],
        [Far(x), mods, *(Far(w) for w in (*wi, *wo))],
        [
            Far(shape((rows, width), bf16)),
            Far(shape((3, rows, width), bf16)),
            Far(shape((frames * heads, n, n), bf16)),
            Far(shape((rows, cols), bf16)),
            Far(shape((rows, cols), bf16)),
            Far(shape((rows, width), bf16)),
            shape((rows // 2, width), bf16),
            shape((rows // 2, width), bf16),
        ],
        [],
        rows * width * (8 * width + 4 * n),
        frames * heads * n * n,
    )


def spatial_back_kernel(
    need, done, side, valid, near, far, cot, mods, qkv, probs, ctx0, ctx1, branch, wo0, wo1,
    grad, rows, dqkv0, dqkv1, dgate,
):
    frames = valid.shape[0] // 2
    n, width = cot.shape[0] // frames, cot.shape[1]
    cols, half = wo0.shape[0], n // 2
    need(0, 1, 2, 3, 8, 9, 10)
    for f in range(frames):
        all_rows = slice(f * n, (f + 1) * n)
        m = Mods(mods, valid, f, 0, width)
        source = slice(f * half, (f + 1) * half)
        here = pl.ds(pl.multiple_of(f * n + side[0] * half, half), half)
        there = pl.ds(pl.multiple_of(f * n + (1 - side[0]) * half, half), half)
        grad[here, :] = near[source, :]
        grad[there, :] = cot[there, :].astype(f32) + far[source, :].astype(f32)
        g = grad[all_rows, :]
        dgate[f : f + 1, :] = column_sum(g * branch[all_rows, :].astype(f32)) * m.valid
        rows[all_rows, :] = (g * m.gate).astype(bf16)
    context_grads = [dot(rows[...], w[...], NT).astype(bf16) for w in (wo0, wo1)]
    need(4, 5, 6, 7)
    for f in range(frames):
        all_rows = slice(f * n, (f + 1) * n)
        for h, (ctx, dqkv) in enumerate(((ctx0, dqkv0), (ctx1, dqkv1))):
            for j in range(cols // LANES):
                low = slice(j * LANES, (j + 1) * LANES)
                at = slice(h * cols + j * LANES, h * cols + (j + 1) * LANES)
                q, k, v = qkv[0, all_rows, at], qkv[1, all_rows, at], qkv[2, all_rows, at]
                d = context_grads[h][all_rows, low]
                product = d.astype(f32) * ctx[all_rows, low].astype(f32)
                delta = jnp.sum(pair_rows(product), -1, keepdims=True)
                head = f * (width // HD) + h * (cols // HD) + 2 * j
                p = jnp.concatenate([probs[head], probs[head + 1]], axis=0)
                d = pair_rows(d)
                ds = (p.astype(f32) * (dot(d, v, NT) - delta)).astype(bf16)
                dv = dot(p, d, TN)
                dq = pair_lanes(dot(ds, k))
                dk = dot(ds, pair_rows(q), TN)
                for i, y in enumerate((dq * SCALE, dk, dv)):
                    to = i * cols + j * LANES
                    dqkv[all_rows, to : to + LANES] = y.astype(bf16)


def spatial_back(side, valid, near, far, cot, mods, qkv, probs, ctx, branch, wo):
    rows, width = cot.shape
    frames, cols = valid.shape[0] // 2, wo[0].shape[0]
    n = rows // frames
    return staged(
        spatial_back_kernel,
        [side, valid],
        [near, far, Far(cot), mods, *(Far(a) for a in (qkv, probs, *ctx, branch, *wo))],
        [
            shape((rows, width), f32),
            shape((rows, width), bf16),
            shape((rows, 3 * cols), bf16),
            shape((rows, 3 * cols), bf16),
            shape((frames, width), f32),
        ],
        [],
        rows * width * (2 * width + 10 * n),
    )


def spatial_input_kernel(
    need, done, side, valid, grad, mods, x, near, far, dqkv0, dqkv1, wi0, wi1, out, layer_out, dmod
):
    frames = valid.shape[0] // 2
    n, width = x.shape[0] // frames, x.shape[1]
    half = n // 2
    need(7, 8)
    inputs = input_sum((dqkv0, dqkv1), (wi0, wi1))
    need(0, 1, 2, 3, 4, 5, 6)
    for f in range(frames):
        m = Mods(mods, valid, f, 0, width)
        here = pl.ds(pl.multiple_of(f * n + side[0] * half, half), half)
        there = pl.ds(pl.multiple_of(f * n + (1 - side[0]) * half, half), half)
        layer_out[here, :] = near[f * half : (f + 1) * half, :]
        layer_out[there, :] = far[f * half : (f + 1) * half, :]
        at = slice(f * n, (f + 1) * n)
        g = inputs[at]
        normed, inv_std = norm(x[at, :].astype(f32))
        dmod[f : f + 1, :width] = column_sum(g)
        dmod[f : f + 1, width:] = column_sum(g * normed)
        out[at, :] = grad[at, :] + norm_back(g, normed, inv_std, m.scale1)
    done(0, 1, 2)


def spatial_input(side, valid, grad, mods, x, near, far, dqkv, wi):
    rows, width = x.shape
    return staged(
        spatial_input_kernel,
        [side, valid],
        [grad, mods, Far(x), Far(near), Far(far), *dqkv, *(Far(w) for w in wi)],
        [
            Far(shape((rows, width), f32)),
            Far(shape((rows, width), bf16)),
            shape((valid.shape[0] // 2, 2 * width), f32),
        ],
        [],
        6 * rows * width * width,
    )


BLOCKS = 16


def store_ordered(order, scratch, keep, send, columns):
    size = scratch.shape[0] // BLOCKS
    for p in range(BLOCKS):
        out = keep if p < BLOCKS // 2 else send
        to = (p % (BLOCKS // 2)) * size
        at = pl.ds(pl.multiple_of(order[p] * size, size), size)
        out[to : to + size, columns] = scratch[at, :]


def weights_kernel(need, done, order, s0, d0, s1, d1, r0, c0, r1, c1, keep, send, wide, narrow):
    split = d0.shape[1]
    need(0, 1)
    total = dot(s0[...], d0[...], TN)
    need(2, 3)
    wide[...] = (total + dot(s1[...], d1[...], TN)).astype(bf16)
    store_ordered(order, wide, keep, send, slice(0, split))
    need(4, 5, 6, 7)
    narrow[...] = (dot(r0[...], c0[...], TN) + dot(r1[...], c1[...], TN)).astype(bf16)
    store_ordered(order, narrow, keep, send, slice(split, keep.shape[1]))
    done(0, 1)


def weights(order, sub, dqkv, rows, ctx):
    n, width = sub[0].shape
    split, cols = dqkv[0].shape[1], ctx[0].shape[1]
    return staged(
        weights_kernel,
        [order],
        [Far(sub[0]), dqkv[0], sub[1], dqkv[1], rows[0], Far(ctx[0]), rows[1], ctx[1]],
        [shape((width // 2, split + cols), bf16)] * 2,
        [pltpu.VMEM((width, split), bf16), pltpu.VMEM((width, cols), bf16)],
        4 * n * width * (split + cols),
    )


def head_sums(products, gather, stack):
    n, count = products[0].shape[0], len(products)
    for i, x in enumerate(products):
        hi = x.astype(bf16)
        stack[i * n : (i + 1) * n, :] = hi
        stack[(count + i) * n : (count + i + 1) * n, :] = (x - hi.astype(f32)).astype(bf16)
    y = dot(stack[...], gather)
    return [y[i * n : (i + 1) * n] + y[(count + i) * n : (count + i + 1) * n] for i in range(count)]


def head_maps(width):
    feature = lax.broadcasted_iota(jnp.int32, (width, LANES), 0) // HD
    head = lax.broadcasted_iota(jnp.int32, (width, LANES), 1)
    gather = (feature == head).astype(bf16)
    feature = lax.broadcasted_iota(jnp.int32, (LANES, width), 1) // HD
    head = lax.broadcasted_iota(jnp.int32, (LANES, width), 0)
    return gather, (feature == head).astype(bf16)


def temporal_kernel(
    need, done, side, valid, bias, x0, x1, b0, b1, mods, wi0, wi1, wo0, wo1,
    stream, sub, qkv, probs, ctx0, ctx1, branch, stream2, sub2, stack, small,
):
    rows, width = sub.shape
    cols, frames = wi0.shape[2], mods.shape[0]
    n = rows // frames
    at = [pl.ds(f * n, n) for f in range(frames)]
    need(0, 1, 2, 3, 4)
    for f in range(frames):
        xs, bs = (x0, b0) if f < frames // 2 else (x1, b1)
        g = f % (frames // 2)
        source = pl.ds(pl.multiple_of((2 * g + side[0]) * n, n), n)
        before, m = Mods(mods, valid, f, 0, width), Mods(mods, valid, f, 1, width)
        s = xs[source, :].astype(f32) + before.gate * bs[at[g], :].astype(f32)
        stream[at[f], :] = s
        normed, _ = norm(s)
        sub[at[f], :] = (normed * m.scale1 + m.shift).astype(bf16)
    done(0, 1)
    need(5, 6)
    project(sub[...], (wi0, wi1), qkv)
    done(2)
    gather, spread = head_maps(width)
    for f in range(frames):
        q = qkv[0, at[f], :].astype(f32)
        scores = head_sums(
            [q * qkv[1, at[g], :].astype(f32) for g in range(frames)], gather, stack
        )
        scores = [s + bias[f, g] for g, s in enumerate(scores)]
        top = functools.reduce(jnp.maximum, scores)
        e = [jnp.exp(s - top) for s in scores]
        inv = 1.0 / sum(e)
        for g in range(frames):
            p = (e[g] * inv).astype(bf16)
            probs[f * frames + g] = p
            small[at[g], :] = p
        spread_p = dot(small[...], spread)
        context = sum(
            spread_p[g * n : (g + 1) * n] * qkv[2, at[g], :].astype(f32) for g in range(frames)
        )
        ctx0[at[f], :] = context[:, :cols].astype(bf16)
        ctx1[at[f], :] = context[:, cols:].astype(bf16)
    done(3, 4, 5)
    need(7, 8)
    for f in range(frames):
        m, after = Mods(mods, valid, f, 1, width), Mods(mods, valid, f, 2, width)
        b = dot(ctx0[at[f], :], wo0[...]) + dot(ctx1[at[f], :], wo1[...])
        branch[at[f], :] = b.astype(bf16)
        s = stream[at[f], :] + m.gate * b
        stream2[at[f], :] = s
        normed, _ = norm(s)
        sub2[at[f], :] = (normed * after.scale1 + after.shift).astype(bf16)
    done(6, 7, 8)


def temporal(side, valid, bias, x0, x1, b0, b1, mods, wi, wo):
    rows, width = x0.shape
    frames, cols = mods.shape[0], wo[0].shape[0]
    n = rows // frames
    return staged(
        temporal_kernel,
        [side, valid, bias],
        [Far(x0), Far(x1), b0, b1, mods, *(Far(w) for w in (*wi, *wo))],
        [
            Far(shape((rows, width), f32)),
            Far(shape((rows, width), bf16)),
            Far(shape((3, rows, width), bf16)),
            Far(shape((frames * frames, n, LANES), bf16)),
            Far(shape((rows, cols), bf16)),
            Far(shape((rows, cols), bf16)),
            Far(shape((rows, width), bf16)),
            Far(shape((rows, width), f32)),
            shape((rows, width), bf16),
        ],
        [pltpu.VMEM((2 * rows, width), bf16), pltpu.VMEM((rows, LANES), bf16)],
        8 * rows * width * width,
        16 * frames * rows,
    )


def temporal_back_kernel(
    need, done, side, valid, ci0, ci1, own, came, mods, stream2, branch, wo0, wo1, qkv, probs,
    wi0, wi1, stream,
    out_near, out_far, rows, dqkv0, dqkv1, grad_near, delta_far, dmod, grad, stack, small,
):
    width, cols, frames = stream.shape[1], wo0.shape[0], mods.shape[0]
    n = stream.shape[0] // frames
    at = [pl.ds(f * n, n) for f in range(frames)]
    gather, spread = head_maps(width)

    def cotangent(f):
        source = ci0 if f < frames // 2 else ci1
        start = (2 * (f % (frames // 2)) + side[0]) * n
        return source[pl.ds(pl.multiple_of(start, n), n), :].astype(f32)

    def put(f, i, value):
        dmod[f : f + 1, i * width : (i + 1) * width] = value

    need(0, 1, 2, 3, 4, 5, 6)
    for f in range(frames):
        m = Mods(mods, valid, f, 2, width)
        s, g = stream2[at[f], :], cotangent(f)
        b = own[0, at[f], :] + came[0, at[f], :].astype(f32)
        d = own[1, at[f], :] + came[1, at[f], :].astype(f32)
        normed, inv_std = norm(s)
        out = out_near if f < frames // 2 else out_far
        out[at[f % (frames // 2)], :] = (s + m.gate * b).astype(bf16)
        put(f, 3, column_sum(d))
        put(f, 4, column_sum(d * normed))
        put(f, 5, column_sum(b * g) * m.valid)
        g = g + norm_back(d, normed, inv_std, m.scale1)
        grad[at[f], :] = g
        m = Mods(mods, valid, f, 1, width)
        put(f, 2, column_sum(g * branch[at[f], :].astype(f32)) * m.valid)
        rows[at[f], :] = (g * m.gate).astype(bf16)
    done(0, 1, 2)
    need(7, 8, 9, 10)
    context_grad = [dot(rows[...], w[...], NT) for w in (wo0, wo1)]

    def store(f, i, value):
        value = value.astype(bf16)
        dqkv0[at[f], i * cols : (i + 1) * cols] = value[:, :cols]
        dqkv1[at[f], i * cols : (i + 1) * cols] = value[:, cols:]

    dk, dv = [0.0] * frames, [0.0] * frames
    for f in range(frames):
        d = jnp.concatenate([c[f * n : (f + 1) * n] for c in context_grad], axis=1)
        d = d.astype(bf16).astype(f32)
        prob_grad = head_sums(
            [d * qkv[2, at[g], :].astype(f32) for g in range(frames)], gather, stack
        )
        p = [probs[f * frames + g] for g in range(frames)]
        p32 = [a.astype(f32) for a in p]
        total = sum(a * b for a, b in zip(prob_grad, p32))
        for g in range(frames):
            small[g * n : (g + 1) * n, :] = (p32[g] * (prob_grad[g] - total)).astype(bf16)
            small[(frames + g) * n : (frames + g + 1) * n, :] = p[g]
        spread_all = dot(small[...], spread)
        q = qkv[0, at[f], :].astype(f32)
        dq = 0.0
        for g in range(frames):
            ds = spread_all[g * n : (g + 1) * n]
            dq = dq + ds * qkv[1, at[g], :].astype(f32)
            dk[g] = dk[g] + ds * q
            dv[g] = dv[g] + spread_all[(frames + g) * n : (frames + g + 1) * n] * d
        store(f, 0, dq * SCALE)
    for g in range(frames):
        store(g, 1, dk[g])
        store(g, 2, dv[g])
    done(3, 4)
    need(11, 12, 13)
    inputs = input_sum((dqkv0, dqkv1), (wi0, wi1))
    for f in range(frames):
        m = Mods(mods, valid, f, 1, width)
        d = inputs[f * n : (f + 1) * n]
        normed, inv_std = norm(stream[at[f], :])
        put(f, 0, column_sum(d))
        put(f, 1, column_sum(d * normed))
        new = grad[at[f], :] + norm_back(d, normed, inv_std, m.scale1)
        if f < frames // 2:
            grad_near[at[f], :] = new
        else:
            delta_far[at[f - frames // 2], :] = (new - cotangent(f)).astype(bf16)
    done(5, 6, 7)


def temporal_back(
    side, valid, ci0, ci1, own, came, mods, stream, stream2, qkv, probs, branch, wi, wo
):
    rows, width = stream.shape
    frames, cols = mods.shape[0], wo[0].shape[0]
    return staged(
        temporal_back_kernel,
        [side, valid],
        [Far(ci0), Far(ci1), own, came, mods]
        + [Far(a) for a in (stream2, branch, *wo, qkv, probs, *wi, stream)],
        [
            Far(shape((rows // 2, width), bf16)),
            Far(shape((rows // 2, width), bf16)),
            shape((rows, width), bf16),
            shape((rows, 3 * cols), bf16),
            shape((rows, 3 * cols), bf16),
            shape((rows // 2, width), f32),
            shape((rows // 2, width), bf16),
            shape((frames, 6 * width), f32),
        ],
        [
            pltpu.VMEM((rows, width), f32),
            pltpu.VMEM((2 * rows, width), bf16),
            pltpu.VMEM((2 * rows, LANES), bf16),
        ],
        8 * rows * width * width,
    )


def gelu_both(u):
    k = 0.7978845608028654
    squared = u * u
    half = 0.5 + 0.5 * jnp.tanh(u * (k + (k * 0.044715) * squared))
    act = u * half
    return act, half + (act * (1.0 - half)) * (2 * k + (6 * k * 0.044715) * squared)


def feed_kernel(
    need, done, side, valid, order, s0, s1, ci0, ci1, mods, wu, wd,
    keep_a, send_a, keep_b, send_b, acc0, away, s, r, acc1, inner, outer,
):
    width, hidden, frames = s0.shape[1], wu.shape[1], mods.shape[0]
    n, chunk, size = s0.shape[0] // frames, inner.shape[1], width // BLOCKS
    total = s0.shape[0]
    acc0[...] = jnp.zeros_like(acc0)
    acc1[...] = jnp.zeros_like(acc1)
    s[:total, :] = s0[...]
    s[total:, :] = s1[...]
    need(0, 1, 2, 3, 4)
    for f in range(frames):
        m = Mods(mods, valid, f, 2, width)
        g = f % (frames // 2)
        source = ci0 if f < frames // 2 else ci1
        here = pl.ds(pl.multiple_of((2 * g + side[0]) * n, n), n)
        there = pl.ds(pl.multiple_of((2 * g + 1 - side[0]) * n, n), n)
        r[f * n : (f + 1) * n, :] = (m.gate * source[here, :].astype(f32)).astype(bf16)
        to = frames + (f + frames // 2) % frames
        r[to * n : (to + 1) * n, :] = (m.gate * source[there, :].astype(f32)).astype(bf16)
    need(5, 6)

    def step(i):
        at = slice(i * chunk, (i + 1) * chunk)
        up, down = wu[:, at], wd[at, :]
        act, slope = gelu_both(dot(s[...], up))
        act = act.astype(bf16)
        pre_grad = (slope * dot(r[...], down, NT)).astype(bf16)
        for j, y in enumerate((dot(act, down), dot(pre_grad, up, NT))):
            acc0[j] += y[:total]
            acc1[j] += y[total:]
        inner[...] = dot(s[...], pre_grad, TN).astype(bf16)
        outer[...] = dot(r[...], act, TN).astype(bf16)
        low = i * chunk
        if low < keep_a.shape[1]:
            keep, send, first, results = keep_a, send_a, 0, (0, 1)
        else:
            keep, send, first, results = keep_b, send_b, BLOCKS, (2, 3)
            low = low - keep_a.shape[1]
        to_columns = slice(low, low + chunk)
        for p in range(BLOCKS):
            out, to = (keep, p) if p < BLOCKS // 2 else (send, p - BLOCKS // 2)
            rows = pl.ds(pl.multiple_of(order[first + p] * size, size), size)
            out[2 * to * size : (2 * to + 1) * size, to_columns] = inner[rows, :]
            out[(2 * to + 1) * size : (2 * to + 2) * size, to_columns] = outer[rows, :]
        done(*results, at=(slice(None), pl.ds(low, chunk)))

    for i in range(hidden // chunk):
        step(i)
    away[...] = acc1[...].astype(bf16)


def feed(side, valid, order, sub, cots, mods, wu, wd):
    rows, width = sub[0].shape
    hidden, chunk = wu.shape[1], 512
    part_b = hidden // 3 // chunk * chunk
    part_a = hidden - part_b
    return staged(
        feed_kernel,
        [side, valid, order],
        [*sub, *(Far(c) for c in cots), mods, Far(wu), Far(wd)],
        [
            Far(shape((width, part_a), bf16)),
            Far(shape((width, part_a), bf16)),
            Far(shape((width, part_b), bf16)),
            Far(shape((width, part_b), bf16)),
            shape((2, rows, width), f32),
            shape((2, rows, width), bf16),
        ],
        [
            pltpu.VMEM((2 * rows, width), bf16),
            pltpu.VMEM((2 * rows, width), bf16),
            pltpu.VMEM((2, rows, width), f32),
            pltpu.VMEM((width, chunk), bf16),
            pltpu.VMEM((width, chunk), bf16),
        ],
        24 * rows * width * hidden,
        2 * rows * hidden,
    )


def condition_kernel(first_block, x, w, out, parts, blocks, sems):
    n, width = x.shape[0], out.shape[0]
    count = x.shape[1] // width
    copies = [
        pltpu.make_async_copy(
            w.at[:, pl.ds((first_block + i) * width, width)], blocks.at[i], sems.at[i]
        )
        for i in range(count)
    ]
    for c in copies:
        c.start()
    total = 0.0
    for i in range(count):
        y = x[:, i * width : (i + 1) * width]
        hi = y.astype(bf16).astype(f32)
        mid = (y - hi).astype(bf16).astype(f32)
        for j, part in enumerate((hi, mid, y - hi - mid, jnp.zeros_like(y))):
            parts[j * n : (j + 1) * n, :] = part
        copies[i].wait()
        total = total + dot(blocks[i], parts[...].astype(bf16), NT)
    out[...] = total


def condition_rows(x, w, first_block):
    n, width = x.shape[0], w.shape[0]
    count = x.shape[1] // width
    out = call(
        functools.partial(condition_kernel, first_block),
        8 * n * width * x.shape[1],
        2 * width * x.shape[1],
        ROOM + 2 * width * x.shape[1],
        in_specs=[VM, pl.BlockSpec(memory_space=pltpu.HBM)],
        out_specs=VM,
        out_shape=shape((width, 4 * n), f32),
        scratch_shapes=[
            pltpu.VMEM((4 * n, width), f32),
            pltpu.VMEM((count, width, width), bf16),
            pltpu.SemaphoreType.DMA((count,)),
        ],
    )(x, in_hbm(w))
    return out.reshape(width, 4, n).sum(axis=1)


def local(
    patches_in, cotangent, condition, frame_clip, frame_valid, w_ada, sp_qkv, sp_out, tm_qkv, tm_out, w_up, w_down,
    dp_size,
):
    frames, patches, width = patches_in.shape
    clips = condition.shape[0]
    t = lax.axis_index("tensor")
    d = lax.axis_index("dp")
    first = t == 0

    def swap(a):
        return lax.ppermute(a, "tensor", [(0, 1), (1, 0)])

    def own_first(a):
        return jnp.where(first, a, jnp.concatenate([a[frames:], a[:frames]], axis=0))

    fence = lax.optimization_barrier
    sq, so, tq, to = ((w, swap(w)) for w in (sp_qkv, sp_out, tm_qkv, tm_out))
    x, cot = patches_in.reshape(-1, width), cotangent.reshape(-1, width)
    x_other, cot_other = swap(x), swap(cot)
    clip_ids = own_first(frame_clip)
    valid_ids = own_first(frame_valid)
    onehot = (clip_ids[:, None] == jnp.arange(clips, dtype=jnp.int32)[None, :]).astype(f32)
    cond_rows = jnp.dot(onehot, condition, precision=highest)
    act_low = jax.nn.silu(cond_rows).astype(bf16)
    mods = jnp.dot(act_low, w_ada, preferred_element_type=f32)
    side, valid = t.reshape(1), valid_ids.astype(f32)
    allowed = (clip_ids[:, None] == clip_ids[None, :]) & (valid_ids[None, :] == 1) | jnp.eye(
        2 * frames, dtype=bool
    )
    bias = jnp.where(allowed, 0.0, -1e30)

    bit0, bit1, rest, outer = d % 2, d // 2 % 2, d // 4, dp_size // 4
    halving = dp_size == BLOCKS
    p = jnp.arange(BLOCKS, dtype=jnp.int32)
    order = order_b = p

    def order_of(far0, far1, z0, z1):
        bx, by = jnp.where(first, far0, far1), jnp.where(first, far1, far0)
        return 4 * (rest ^ (z0 + 2 * z1)) + 2 * (bit1 ^ by) + (bit0 ^ bx)

    if halving:
        bits = [p // 8, p // 4 % 2, p // 2 % 2, p % 2]
        order = order_of(*bits)
        order_b = order_of(bits[1], bits[2], bits[0], bits[3])
    feed_order = jnp.concatenate([order, order_b])

    def both_cores(first_bit, second_bit):
        return [(2 * i, 2 * (i ^ first_bit)) for i in range(dp_size)] + [
            (2 * i + 1, 2 * (i ^ second_bit) + 1) for i in range(dp_size)
        ]

    def flip(bits):
        return [(i, i ^ bits) for i in range(dp_size)]

    def across(a, which):
        if not halving:
            return a
        if which < 2:
            pairs = both_cores(*((1, 2) if which == 0 else (2, 1)))
            return lax.ppermute(a, ("dp", "tensor"), pairs)
        return lax.ppermute(a, "dp", flip(4 if which == 2 else 8))

    def fold(keep, came):
        if not halving:
            return keep, came
        n = keep.shape[0] // 2
        return keep[:n] + came[:n], keep[n:] + came[n:]

    def gather_z(keep, came):
        if not halving:
            return [keep, came]
        n = keep.shape[0] // 4
        return [keep[i * n : (i + 1) * n] + came[i * n : (i + 1) * n] for i in range(4)]

    def spread_z(pieces):
        if not halving:
            return pieces
        return pieces[:1] + [
            lax.ppermute(pieces[i], "dp", flip(4 * k)) for i, k in ((2, 1), (1, 2), (3, 3))
        ]

    def finish(pieces):
        if not halving:
            a = jnp.concatenate(pieces, axis=0).astype(f32)
            return lax.psum_scatter(a, "dp", scatter_dimension=0, tiled=True)
        return sum(a.astype(f32) for a in pieces)

    def feed_finish(*parts):
        if halving:
            a = jnp.concatenate([finish(pieces) for pieces in parts], axis=1)
            return a.reshape(2, width // dp_size, -1)
        a = jnp.concatenate([jnp.concatenate(pieces, axis=0) for pieces in parts], axis=1)
        a = a.astype(f32).reshape(BLOCKS, 2, width // BLOCKS, -1)
        a = a.transpose(1, 0, 2, 3).reshape(2, width, -1)
        return lax.psum_scatter(a, "dp", scatter_dimension=1, tiled=True)

    sub0, qkv0, probs0, *ctx0, branch0, near, far = spatial(
        side, valid, x, mods, sq, so
    )
    stream1, sub1, qkv1, probs1, *ctx1, branch1, stream2, sub2 = temporal(
        side, valid, bias, x, x_other, near, swap(far), mods, tq, to
    )
    mk, ms, nk, ns, sum0, away = feed(
        side, valid, feed_order, (sub2, swap(sub2)), (cot, cot_other), mods, w_up, w_down
    )
    early = [swap(a) for a in (sub1, ctx1[1])]
    early, away = fence((early, away))
    mr, nr = across(ms, 0), across(ns, 2)
    out_near, out_far, rows1, *dqkv1, grad_near, delta, dmod12 = temporal_back(
        side, valid, cot, cot_other, sum0, swap(away), mods, stream1, stream2, qkv1, probs1,
        branch1, tq, to,
    )
    came1 = [early[0], swap(dqkv1[1]), swap(rows1), early[1]]
    delta, nr = fence((swap(delta), nr))
    nk, ns = fold(nk, nr)
    ns, delta = fence((ns, delta))
    nr = across(ns, 0)
    grad, rows0, *dqkv0, dgate0 = spatial_back(
        side, valid, grad_near, delta, cot, mods, qkv0, probs0, ctx0, branch0, so
    )
    came0 = [swap(a) for a in (sub0, dqkv0[1], rows0, ctx0[1])]
    came1, mr, nr, dqkv0 = fence((came1, mr, nr, dqkv0))
    mk, ms = fold(mk, mr)
    nk, ns = fold(nk, nr)
    ms, ns, came1 = fence((ms, ns, came1))
    mr, nr = across(ms, 1), across(ns, 1)
    tk, ts = weights(
        order, (sub1, came1[0]), (dqkv1[0], came1[1]), (rows1, came1[2]), (ctx1[0], came1[3])
    )
    tr = across(ts, 0)
    came0, mr, ts = fence((came0, mr, ts))
    mk, ms = fold(mk, mr)
    ms, came0 = fence((ms, came0))
    mr = across(ms, 2)
    sk, ss = weights(
        order, (sub0, came0[0]), (dqkv0[0], came0[1]), (rows0, came0[2]), (ctx0[0], came0[3])
    )
    sr = across(ss, 0)
    mr, nr, ss = fence((mr, nr, ss))
    mk, ms = fold(mk, mr)
    nk, ns = fold(nk, nr)
    ms, ns, ss, grad = fence((ms, ns, ss, grad))
    mr, nr = across(ms, 3), across(ns, 3)
    grad, patches_out, dmod0 = spatial_input(
        side, valid, grad, mods, x, out_near, swap(out_far), dqkv0, sq
    )
    tr, dmod0 = fence((tr, dmod0))
    tk, ts = fold(tk, tr)
    ts, dmod0 = fence((ts, dmod0))
    tr = across(ts, 1)
    late = jnp.concatenate([dmod0, dgate0], axis=1)
    mine = jnp.concatenate([late, dmod12[:frames] + swap(dmod12[frames:])], axis=1)
    act_grad = condition_rows(mine, w_ada, 0).T
    unused, silu_back = jax.vjp(jax.nn.silu, cond_rows[:frames])
    cond_term = silu_back(act_grad)[0]
    devices = 2 * dp_size
    own_ids = clip_ids[:frames].astype(f32)
    payload = jnp.concatenate(
        [
            mine.reshape(frames, devices, -1),
            cond_term.reshape(frames, devices, -1),
            jnp.broadcast_to(own_ids[:, None, None], (frames, devices, 1)),
        ],
        axis=2,
    )
    got = lax.all_to_all(
        payload.transpose(1, 0, 2), ("dp", "tensor"), split_axis=0, concat_axis=0, tiled=True
    ).reshape(devices * frames, -1)
    tr, sr, mr, nr, act_grad = fence((tr, sr, mr, nr, act_grad))
    sk, ss = fold(sk, sr)
    tk, ts = fold(tk, tr)
    sr, tr = across(ss, 1), across(ts, 2)
    sr, tr, got = fence((sr, tr, got))
    pieces = gather_z(sk, sr)
    tk, ts = fold(tk, tr)
    pieces, ts, mk, mr, nk, nr, got = fence((pieces, ts, mk, mr, nk, nr, got))
    s4, tr = spread_z(pieces), across(ts, 3)
    ada_cols = 9 * width // devices
    ids = got[:, -1].astype(jnp.int32)
    every = (ids[:, None] == jnp.arange(clips, dtype=jnp.int32)[None, :]).astype(f32)
    act_all = jnp.dot(
        every, jax.nn.silu(condition).astype(bf16).astype(f32), precision=highest
    )
    ada_grad = jnp.dot(act_all.T, got[:, :ada_cols], precision=highest)
    condition_grad = jnp.dot(every.T, got[:, ada_cols:-1], precision=highest)

    def attention_grads(a):
        a = a.reshape(a.shape[0], 4, -1).transpose(1, 0, 2)
        return a[:3], a[3].T

    up_out, down_out = feed_finish([mk, mr], [nk, nr])
    return (
        patches_out.reshape(patches_in.shape),
        grad.reshape(patches_in.shape),
        condition_grad,
        ada_grad,
        *attention_grads(finish(s4)),
        *attention_grads(finish([tk, tr])),
        up_out,
        down_out.T,
    )


def solution(mesh):
    return jax.shard_map(
        functools.partial(local, dp_size=mesh.shape["dp"]),
        mesh=mesh,
        in_specs=(
            P(("dp", "tensor"), None, None),
            P(("dp", "tensor"), None, None),
            P(),
            P("dp"),
            P("dp"),
            P(),
            P(None, None, "tensor"),
            P("tensor", None),
            P(None, None, "tensor"),
            P("tensor", None),
            P(None, "tensor"),
            P("tensor", None),
        ),
        out_specs=(
            P(("dp", "tensor"), None, None),
            P(("dp", "tensor"), None, None),
            P(None, ("dp", "tensor")),
            P(None, ("dp", "tensor")),
            P(None, "dp", "tensor"),
            P("tensor", "dp"),
            P(None, "dp", "tensor"),
            P("tensor", "dp"),
            P("dp", "tensor"),
            P("tensor", "dp"),
        ),
        check_vma=False,
    )
```
